256 devices in a mesh: rep: 32 (over y, x, z_hi), shard: 8 (over z_lo, core).
Axes of the slice: x: 4, y: 4, z: 8 (z_hi: 2, z_lo: 4; z = z_hi * 4 + z_lo), core: 2. Of those that a mesh axis runs over, the one named last changes fastest.
Arguments:
- x_in: bfloat16 [49152, 6144], P(('rep', 'shard')), may hold values from -6 to 6
- attn_out: bfloat16 [49152, 6144], P(('rep', 'shard')), may hold values from -6 to 6
- grads_out: bfloat16 [49152, 512], P(('rep', 'shard')), may hold values from -0.18042196 to 0.18042196
- master: float32 [128, 24576], P('shard'), may hold values from -0.51031036 to 0.51031036
- moment: float32 [128, 24576], P('shard'), may hold values from -3 to 3
- second: float32 [128, 24576], P('shard'), may hold values from 0.05 to 2
Outputs:
- new_master: float32 [128, 24576], P('shard')
- new_moment: float32 [128, 24576], P('shard')
- new_second: float32 [128, 24576], P('shard')
- gathered: bfloat16 [128, 24576], replicated
The draws below stay inside these ranges and needn't reach their ends.
All inputs are finite; a program needn't handle non-finite values.
Results may differ from the reference program's by a relative error of at most 0.0004.
Values may be sent and summed in bfloat16 or wider, within the bound.
No kernel may reach another device: no remote copies, remote signals or barrier semaphores. Data moves between devices by JAX's collectives and lax.ppermute only.
A program may use at most 128 MiB of HBM per device.

```python
import math
import jax
import jax.numpy as jnp
from jax import lax

D = 6144
TOK_DEV = 192
ROWS_DEV = 16
WROWS = 128
TOKENS = 49152


def draw_master(key, part):
    key = jax.random.fold_in(key, 11)
    key_row, key_col, key_base = jax.random.split(key, 3)
    row_factor = jnp.exp(jax.random.uniform(key_row, (WROWS, 1), jnp.float32, -1.15, 1.15))
    col_factor = jnp.exp(jax.random.uniform(key_col, (1, 4 * D), jnp.float32, -1.15, 1.15))
    base = jnp.clip(jax.random.normal(key_base, (WROWS, 4 * D), jnp.float32), -3.9, 3.9)
    return (base * row_factor * col_factor * D ** (-0.5)).astype(jnp.float32)


def draw_grads_out(key, part):
    key = jax.random.fold_in(key, 23)
    key_pair, key_base = jax.random.split(key, 2)
    block_count = WROWS // ROWS_DEV
    pairing = jax.random.permutation(key_pair, block_count)
    token_block = jnp.arange(TOKENS, dtype=jnp.int32) // TOK_DEV % block_count
    column_block = jnp.arange(4 * WROWS, dtype=jnp.int32) // (4 * ROWS_DEV)
    matched = pairing[token_block][:, None] == column_block[None, :]
    factor = jnp.where(matched, 3.0, 1.0).astype(jnp.float32)
    base = jnp.clip(jax.random.normal(key_base, (TOKENS, 4 * WROWS), jnp.float32), -4.0, 4.0)
    return (base * factor * TOKENS ** (-0.5)).astype(jnp.bfloat16)


def levels(own_key, extent, pieces, least, largest):
    level = 1.0
    for axis_at, parts in pieces:
        steps = jax.random.uniform(jax.random.fold_in(jax.random.fold_in(own_key, 6), axis_at), (parts,), jnp.float32, least / len(pieces), largest / len(pieces))
        level = level * jnp.repeat(jnp.exp(steps), extent[axis_at] // parts).reshape((-1,) + (1,) * (len(extent) - 1 - axis_at))
    return level


def centred(own_key, extent, spread, limit, cuts=(), kind=jnp.bfloat16):
    values = spread * jax.random.normal(own_key, extent, jnp.float32)
    if cuts:
        values = values * levels(own_key, extent, cuts, -0.22, 0.18)
    return jnp.clip(values, -limit, limit).astype(kind)


def setup_inputs(seed: int = 0) -> dict:
    splits = jax.random.split(jax.random.key(seed), 7)
    x_in = centred(splits[0], (TOKENS, D), 1.0, 6.0, ((0, 256),))
    attn_out = centred(splits[1], (TOKENS, D), 1.0, 6.0, ((0, 256),))
    grads_out = draw_grads_out(jax.random.fold_in(splits[6], 71), 0)
    master = draw_master(jax.random.fold_in(splits[6], 71), 0)
    moment = centred(splits[4], (WROWS, 4 * D), 0.3, 3.0, ((0, 8),), jnp.float32)
    second = jnp.clip(jnp.exp(math.log(2.0) - 3.6888794 * jax.random.uniform(splits[5], (WROWS, 4 * D), jnp.float32) ** levels(splits[5], (WROWS, 4 * D), ((0, 8),), -0.2, 0.2)), 0.05, 2.0)
    return {"x_in": x_in, "attn_out": attn_out, "grads_out": grads_out, "master": master, "moment": moment, "second": second}


beta_one = 0.9
beta_two = 0.95
learn_rate = 0.002
bias_one = 1.0 - 0.9 ** 10
bias_two = 1.0 - 0.95 ** 10

def reference(x_in, attn_out, grads_out, master, moment, second):
    cotangent = grads_out.reshape(TOKENS, WROWS, 4)
    blocks = []
    for which in range(4):
        source = x_in if which < 3 else attn_out
        blocks.append(jnp.dot(cotangent[:, :, which].T, source, preferred_element_type=jnp.float32))
    gradient = jnp.concatenate(blocks, axis=1)
    new_moment = beta_one * moment + (1.0 - beta_one) * gradient
    new_second = beta_two * second + (1.0 - beta_two) * gradient * gradient
    stepped = master - learn_rate * (new_moment / bias_one) / (jnp.sqrt(new_second / bias_two) + 1e-08)
    shaped = stepped.reshape(WROWS, 4, D)
    scale_rows = jnp.sqrt(lax.optimization_barrier(jnp.sum(shaped * shaped, axis=2, keepdims=True)) + 1e-06)
    new_master = (shaped / scale_rows).reshape(WROWS, 4 * D)
    return (new_master, new_moment, new_second, new_master.astype(jnp.bfloat16))
```

```python
import functools

import jax
import jax.numpy as jnp
from jax import lax
from jax.experimental import pallas as pl
from jax.experimental.pallas import tpu as pltpu
from jax.sharding import Mesh
from jax.sharding import PartitionSpec as P

beta_one = 0.9
beta_two = 0.95
learn_rate = 0.002
bias_one = 1.0 - 0.9**10
bias_two = 1.0 - 0.95**10

REP = ("y", "x", "zh")
SHARD = ("zl", "c")
NY, NX, NZH, NZL, NC = 4, 4, 2, 4, 2
PLANE = NY * NX
PROJ = 4
SEND_SCALE = 128.0
UNIT_SCALE = 32768.0


def adam_update(gradient, master, moment, second):
    new_moment = beta_one * moment + (1.0 - beta_one) * gradient
    new_second = beta_two * second + (1.0 - beta_two) * gradient * gradient
    stepped = master - learn_rate * (new_moment / bias_one) / (
        jnp.sqrt(new_second / bias_two) + 1e-08
    )
    return (stepped, new_moment, new_second)


def terms_kernel(core_ref, g0_ref, g1_ref, x0_ref, x1_ref, a0_ref, a1_ref, out_ref, left_ref):
    rows = out_ref.shape[0]
    tokens, columns = g0_ref.shape

    @pl.when(pl.program_id(0) == 0)
    def _():
        m = lax.broadcasted_iota(jnp.int32, (rows, columns), 0)
        j = lax.broadcasted_iota(jnp.int32, (rows, columns), 1)
        k = m & 3
        want = 128 * ((m >> 2) & 3) + 64 * core_ref[0] + 4 * (m >> 4) + k
        pick = jnp.where(j == want, 1.0, 0.0)
        for which in range(2):
            keep = (k == 3) if which else (k < 3)
            chosen = jnp.where(keep, pick, 0.0).astype(jnp.bfloat16)
            for at, g_ref in enumerate((g0_ref, g1_ref)):
                left_ref[2 * which + at] = lax.dot_general(
                    chosen, g_ref[...], (((1,), (1,)), ((), ())), preferred_element_type=jnp.float32
                ).astype(jnp.bfloat16)

    total = jnp.dot(left_ref[0], x0_ref[...], preferred_element_type=jnp.float32)
    total += jnp.dot(left_ref[1], x1_ref[...], preferred_element_type=jnp.float32)
    total += jnp.dot(left_ref[2], a0_ref[...], preferred_element_type=jnp.float32)
    total += jnp.dot(left_ref[3], a1_ref[...], preferred_element_type=jnp.float32)
    out_ref[...] = total * SEND_SCALE


def terms(core, g0, g1, x0, x1, a0, a1, tile=1024):
    tokens, width = x0.shape
    rows = g0.shape[1] // NC
    whole = pl.BlockSpec(g0.shape, lambda j: (0, 0))
    block = pl.BlockSpec((tokens, tile), lambda j: (0, j))
    return pl.pallas_call(
        terms_kernel,
        grid=(width // tile,),
        in_specs=[pl.BlockSpec(memory_space=pltpu.SMEM), whole, whole, block, block, block, block],
        out_specs=pl.BlockSpec((rows, tile), lambda j: (0, j)),
        out_shape=jax.ShapeDtypeStruct((rows, width), jnp.float32),
        scratch_shapes=[pltpu.VMEM((4, rows, tokens), jnp.bfloat16)],
        compiler_params=pltpu.CompilerParams(vmem_limit_bytes=32 * 2**20),
        cost_estimate=pl.CostEstimate(
            flops=8 * rows * tokens * width, bytes_accessed=10 * tokens * width, transcendentals=0
        ),
        name="terms",
    )(core, g0, g1, x0, x1, a0, a1)


def step_kernel(u_ref, master_ref, moment_ref, second_ref, nm_ref, mo_ref, se_ref, grad_ref):
    k = pl.program_id(0)
    rows, width = master_ref.shape

    @pl.when(k == 0)
    def _():
        parts = u_ref.shape[0]
        m = lax.broadcasted_iota(jnp.int32, (PROJ * rows, parts), 0)
        j = lax.broadcasted_iota(jnp.int32, (PROJ * rows, parts), 1)
        first = (m & 15) * 24 + 16 + (m >> 4)
        pick = jnp.where((j == first) | (j == first + PROJ), 1.0, 0.0).astype(jnp.bfloat16)
        grad_ref[...] = jnp.dot(
            pick, u_ref[...], preferred_element_type=jnp.float32
        )

    gradient = grad_ref[pl.ds(pl.multiple_of(k * rows, rows), rows), :]
    stepped, new_moment, new_second = adam_update(
        gradient, master_ref[...], moment_ref[...], second_ref[...]
    )
    mo_ref[...] = new_moment
    se_ref[...] = new_second
    scale = jnp.sqrt(jnp.sum(stepped * stepped, axis=1, keepdims=True) + 1e-06)
    nm_ref[...] = stepped / scale


def step(u, master, moment, second):
    rows, width = master.shape
    width //= PROJ
    block = pl.BlockSpec((rows, width), lambda k: (0, k))
    return pl.pallas_call(
        step_kernel,
        grid=(PROJ,),
        in_specs=[pl.BlockSpec(u.shape, lambda k: (0, 0)), block, block, block],
        out_specs=[block, block, block],
        out_shape=[jax.ShapeDtypeStruct(master.shape, jnp.float32)] * 3,
        scratch_shapes=[pltpu.VMEM((PROJ * rows, width), jnp.float32)],
        compiler_params=pltpu.CompilerParams(vmem_limit_bytes=40 * 2**20),
        cost_estimate=pl.CostEstimate(
            flops=2 * 64 * 384 * width, bytes_accessed=24 * rows * width * PROJ, transcendentals=0
        ),
        name="step",
    )(u, master, moment, second)


def lay_kernel(core_ref, own_ref, other_ref, out_ref):
    j = pl.program_id(0)
    parts, tile = own_ref.shape
    width = tile * pl.num_programs(0)
    m = lax.broadcasted_iota(jnp.int32, (256, parts), 0)
    n = lax.broadcasted_iota(jnp.int32, (256, parts), 1)
    pick = jnp.where(n == (m & 15) * 24 + ((m >> 4) & 3) * 4 + (m >> 6), 1.0, 0.0)
    pick = pick.astype(jnp.bfloat16)

    def rows_of(ref):
        picked = jnp.dot(pick, ref[...], preferred_element_type=jnp.float32)
        return (picked * (1.0 / UNIT_SCALE)).astype(out_ref.dtype)

    own, other = rows_of(own_ref), rows_of(other_ref)
    mine = core_ref[0] == 0
    low, high = jnp.where(mine, own, other), jnp.where(mine, other, own)
    for k in range(PROJ):
        at = pl.ds(pl.multiple_of(k * width + j * tile, 128), tile)
        for zl in range(NZL):
            part = slice(64 * k + 16 * zl, 64 * k + 16 * zl + 16)
            out_ref[32 * zl : 32 * zl + 16, at] = low[part]
            out_ref[32 * zl + 16 : 32 * zl + 32, at] = high[part]


def lay(core, own, other, rows, tile=1024):
    parts, width = own.shape
    block = pl.BlockSpec((parts, tile), lambda j: (0, j))
    return pl.pallas_call(
        lay_kernel,
        grid=(width // tile,),
        in_specs=[pl.BlockSpec(memory_space=pltpu.SMEM), block, block],
        out_specs=pl.BlockSpec((rows, PROJ * width), lambda j: (0, 0)),
        out_shape=jax.ShapeDtypeStruct((rows, PROJ * width), jnp.bfloat16),
        compiler_params=pltpu.CompilerParams(vmem_limit_bytes=40 * 2**20),
        cost_estimate=pl.CostEstimate(
            flops=4 * 256 * parts * width, bytes_accessed=8 * parts * width, transcendentals=0
        ),
        name="lay",
    )(core, own, other)


def shards(x_in, attn_out, grads_out, master, moment, second):
    width = x_in.shape[1]
    swap = [(0, 1), (1, 0)]
    core = lax.axis_index("c").reshape(1).astype(jnp.int32)
    x_other = lax.ppermute(x_in, "c", swap)
    g_other = lax.ppermute(grads_out, "c", swap)
    a_other = lax.ppermute(attn_out, "c", swap)
    sent = terms(core, grads_out, g_other, x_in, x_other, attn_out, a_other)
    with jax.named_scope("plane_sum"):
        came = lax.all_to_all(
            sent.astype(jnp.float16).reshape(PLANE, NZL * PROJ, width), ("y", "x"), 0, 0, tiled=True
        )
        part = jnp.sum(came.astype(jnp.float32), axis=0) * (1.0 / SEND_SCALE)
    with jax.named_scope("depth_sum"):
        came = lax.all_to_all(part.reshape(NZL, PROJ, width), "zl", 0, 0, tiled=True)
        half = jnp.sum(came, axis=0)
        gradient = half + lax.ppermute(half, "zh", swap)
    with jax.named_scope("own_row"):
        row = lax.axis_index("y") * NX + lax.axis_index("x")

        def piece(a):
            return lax.dynamic_slice(a, (row, 0), (1, PROJ * width)).reshape(PROJ, width)

        stepped, _, _ = adam_update(gradient, piece(master), piece(moment), piece(second))
        scale = jnp.sqrt(jnp.sum(stepped * stepped, axis=1, keepdims=True) + 1e-06)
        unit = lax.reduce_precision(stepped / scale, 8, 7)
        unit = (unit * UNIT_SCALE).astype(jnp.float16)
        coarse = lax.reduce_precision(gradient, 8, 7)
        fine = (gradient - coarse).astype(jnp.float16)
        coarse = coarse.astype(jnp.float16)
    with jax.named_scope("depth_gather"):
        units = lax.all_to_all(
            jnp.broadcast_to(unit[None], (NZL, PROJ, width)), "zl", 0, 0, tiled=True
        )
    with jax.named_scope("plane_gather"):
        payload = jnp.concatenate([units.reshape(NZL * PROJ, width), coarse, fine], axis=0)
        own = lax.all_gather(payload, ("y", "x"), axis=0, tiled=True).astype(jnp.bfloat16)
    other = lax.ppermute(own, "c", swap)
    new_master, new_moment, new_second = step(own, master, moment, second)
    gathered = lay(core, own, other, NZL * NC * master.shape[0])
    return (new_master, new_moment, new_second, gathered)


def solution(mesh):
    fine = Mesh(mesh.devices.reshape(NY, NX, NZH, NZL, NC), REP + SHARD)
    tokens = P(REP + SHARD, None)
    rows = P(SHARD, None)
    return jax.shard_map(
        shards,
        mesh=fine,
        in_specs=(tokens, tokens, tokens, rows, rows, rows),
        out_specs=(rows, rows, rows, P()),
        check_vma=False,
    )
```

```python
import functools

import jax
import jax.numpy as jnp
from jax import lax
from jax.experimental import pallas as pl
from jax.experimental.pallas import tpu as pltpu
from jax.sharding import Mesh
from jax.sharding import PartitionSpec as P

beta_one = 0.9
beta_two = 0.95
learn_rate = 0.002
bias_one = 1.0 - 0.9**10
bias_two = 1.0 - 0.95**10

REP = ("y", "x", "zh")
SHARD = ("zl", "c")
NY, NX, NZH, NZL, NC = 4, 4, 2, 4, 2
PLANE = NY * NX
PROJ = 4
SEND_SCALE = 128.0
UNIT_SCALE = 32768.0


def adam_update(gradient, master, moment, second):
    new_moment = beta_one * moment + (1.0 - beta_one) * gradient
    new_second = beta_two * second + (1.0 - beta_two) * gradient * gradient
    stepped = master - learn_rate * (new_moment / bias_one) / (
        jnp.sqrt(new_second / bias_two) + 1e-08
    )
    return (stepped, new_moment, new_second)


def pick_rows(place_ref, g_ref, left_ref, x_first):
    shape = (left_ref.shape[1], g_ref.shape[1])
    m = lax.broadcasted_iota(jnp.int32, shape, 0)
    j = lax.broadcasted_iota(jnp.int32, shape, 1)
    k = m & 3
    first, second = m >> 6, (m >> 4) & 3
    along_x, along_y = (first, second) if x_first else (second, first)
    i = 4 * ((place_ref[3] + along_y) & 3) + ((place_ref[2] + along_x) & 3)
    want = 128 * ((place_ref[1] + (m >> 2)) & 3) + 64 * place_ref[0] + 4 * i + k
    for at, mine in enumerate((k < 3, k == 3)):
        chosen = jnp.where((j == want) & mine, 1.0, 0.0).astype(jnp.bfloat16)
        left_ref[at] = lax.dot_general(
            chosen, g_ref[...], (((1,), (1,)), ((), ())), preferred_element_type=jnp.float32
        ).astype(jnp.bfloat16)


def two_dots(left_ref, x_ref, a_ref):
    total = jnp.dot(left_ref[0], x_ref[...], preferred_element_type=jnp.float32)
    return total + jnp.dot(left_ref[1], a_ref[...], preferred_element_type=jnp.float32)


def own_kernel(x_first, place_ref, g_ref, x_ref, a_ref, out_ref, left_ref):
    @pl.when(pl.program_id(0) == 0)
    def _():
        pick_rows(place_ref, g_ref, left_ref, x_first)

    out_ref[...] = two_dots(left_ref, x_ref, a_ref)


def other_kernel(x_first, place_ref, g_ref, x_ref, a_ref, base_ref, out_ref, left_ref):
    @pl.when(pl.program_id(0) == 0)
    def _():
        pick_rows(place_ref, g_ref, left_ref, x_first)

    out_ref[...] = (two_dots(left_ref, x_ref, a_ref) + base_ref[...]) * SEND_SCALE


def terms(x_first, place, g, x, a, base=None, tile=1024):
    tokens, width = x.shape
    width //= 2
    rows = g.shape[1] // NC
    skip = 0 if x_first else width // tile
    block = pl.BlockSpec((tokens, tile), lambda j: (0, skip + j))
    result = pl.BlockSpec((rows, tile), lambda j: (0, j))
    bases = [] if base is None else [base]
    return pl.pallas_call(
        functools.partial(own_kernel if base is None else other_kernel, x_first),
        grid=(width // tile,),
        in_specs=[
            pl.BlockSpec(memory_space=pltpu.SMEM),
            pl.BlockSpec(g.shape, lambda j: (0, 0)),
            block,
            block,
        ]
        + [result] * len(bases),
        out_specs=result,
        out_shape=jax.ShapeDtypeStruct((rows, width), jnp.float32),
        scratch_shapes=[pltpu.VMEM((2, rows, tokens), jnp.bfloat16)],
        compiler_params=pltpu.CompilerParams(vmem_limit_bytes=24 * 2**20),
        cost_estimate=pl.CostEstimate(
            flops=4 * rows * tokens * width, bytes_accessed=8 * tokens * width, transcendentals=0
        ),
        name="own_terms" if base is None else "pair_terms",
    )(place, g, x, a, *bases)


def step_kernel(u_ref, master_ref, moment_ref, second_ref, nm_ref, mo_ref, se_ref, grad_ref):
    k = pl.program_id(0)
    rows, width = master_ref.shape

    @pl.when(k == 0)
    def _():
        parts = u_ref.shape[0]
        m = lax.broadcasted_iota(jnp.int32, (PROJ * rows, parts), 0)
        j = lax.broadcasted_iota(jnp.int32, (PROJ * rows, parts), 1)
        first = (m & 15) * 2 * PROJ + (m >> 4)
        pick = jnp.where((j == first) | (j == first + PROJ), 1.0, 0.0).astype(jnp.bfloat16)
        grad_ref[...] = jnp.dot(
            pick, u_ref[...], preferred_element_type=jnp.float32
        )

    gradient = grad_ref[pl.ds(pl.multiple_of(k * rows, rows), rows), :]
    stepped, new_moment, new_second = adam_update(
        gradient, master_ref[...], moment_ref[...], second_ref[...]
    )
    mo_ref[...] = new_moment
    se_ref[...] = new_second
    scale = jnp.sqrt(jnp.sum(stepped * stepped, axis=1, keepdims=True) + 1e-06)
    nm_ref[...] = stepped / scale


def step(u, master, moment, second):
    rows, width = master.shape
    width //= PROJ
    block = pl.BlockSpec((rows, width), lambda k: (0, k))
    return pl.pallas_call(
        step_kernel,
        grid=(PROJ,),
        in_specs=[pl.BlockSpec(u.shape, lambda k: (0, 0)), block, block, block],
        out_specs=[block, block, block],
        out_shape=[jax.ShapeDtypeStruct(master.shape, jnp.float32)] * 3,
        scratch_shapes=[pltpu.VMEM((PROJ * rows, width), jnp.float32)],
        compiler_params=pltpu.CompilerParams(vmem_limit_bytes=40 * 2**20),
        cost_estimate=pl.CostEstimate(
            flops=2 * 64 * 128 * width, bytes_accessed=24 * rows * width * PROJ, transcendentals=0
        ),
        name="step",
    )(u, master, moment, second)


def lay_kernel(place_ref, own_ref, other_ref, out_ref, held_ref, sems):
    j = pl.program_id(0)
    last = pl.num_programs(0) - 1
    parts, tile = own_ref.shape
    width = tile * (last + 1)
    slot = lax.rem(j, 2)

    def copies(step, slot):
        for k in range(PROJ):
            at = pl.ds(pl.multiple_of(k * width + step * tile, 128), tile)
            yield pltpu.make_async_copy(held_ref.at[slot, k], out_ref.at[:, at], sems.at[slot, k])

    @pl.when(j >= 2)
    def _():
        for copy in copies(j - 2, slot):
            copy.wait()

    m = lax.broadcasted_iota(jnp.int32, (256, parts), 0)
    n = lax.broadcasted_iota(jnp.int32, (256, parts), 1)
    wanted = n == (m & 15) * 16 + ((m >> 4) & 3) * 4 + (m >> 6)
    pick = jnp.where(wanted, 1.0 / UNIT_SCALE, 0.0).astype(jnp.bfloat16)
    for ref, core in ((own_ref, place_ref[0]), (other_ref, 1 - place_ref[0])):
        rows = jnp.dot(pick, ref[...], preferred_element_type=jnp.float32).astype(out_ref.dtype)
        for k in range(PROJ):
            for zl in range(NZL):
                to = pl.ds(pl.multiple_of(32 * zl + 16 * core, 16), 16)
                held_ref[slot, k, to] = rows[64 * k + 16 * zl : 64 * k + 16 * zl + 16]
    for copy in copies(j, slot):
        copy.start()

    @pl.when(j == last)
    def _():
        for copy in copies(j - 1, 1 - slot):
            copy.wait()
        for copy in copies(j, slot):
            copy.wait()


def lay(place, own, other, rows, tile=1024):
    parts, width = own.shape
    block = pl.BlockSpec((parts, tile), lambda j: (0, j))
    return pl.pallas_call(
        lay_kernel,
        grid=(width // tile,),
        in_specs=[pl.BlockSpec(memory_space=pltpu.SMEM), block, block],
        out_specs=pl.BlockSpec(memory_space=pl.ANY),
        out_shape=jax.ShapeDtypeStruct((rows, PROJ * width), jnp.bfloat16),
        scratch_shapes=[
            pltpu.VMEM((2, PROJ, rows, tile), jnp.bfloat16),
            pltpu.SemaphoreType.DMA((2, PROJ)),
        ],
        compiler_params=pltpu.CompilerParams(vmem_limit_bytes=24 * 2**20),
        cost_estimate=pl.CostEstimate(
            flops=4 * 256 * parts * width, bytes_accessed=8 * parts * width, transcendentals=0
        ),
        name="lay",
    )(place, own, other)


def shards(x_in, attn_out, grads_out, master, moment, second):
    width = x_in.shape[1]
    swap = [(0, 1), (1, 0)]
    place = jnp.stack([lax.axis_index(name) for name in ("c", "zl", "x", "y")]).astype(jnp.int32)
    half = width // 2

    def along(a, axis, by):
        return lax.ppermute(a, axis, [(i, (i + by) % 4) for i in range(4)])

    def ahead(a, by):
        ring = NZH * NZL
        return lax.ppermute(a, ("zh", "zl"), [(z, (z + by) % ring) for z in range(ring)])

    def shared(blocks, axis, scale):
        sent = (blocks[1:] * scale).astype(jnp.float16)
        came = [along(sent[n - 1], axis, n).astype(jnp.float32) for n in (1, 3, 2)]
        return blocks[0] * scale + came[0] + came[1] + came[2]

    with jax.named_scope("pair"):
        g_other = lax.ppermute(grads_out, "c", swap)
        x_other = lax.ppermute(x_in, "c", swap)
        a_other = lax.ppermute(attn_out, "c", swap)
        first = terms(True, place, grads_out, x_in, attn_out)
        first, place = lax.optimization_barrier((first, place))
        second_half = terms(False, place, grads_out, x_in, attn_out)
        second_half, place = lax.optimization_barrier((second_half, place))
    with jax.named_scope("first"):
        first = terms(True, place, g_other, x_other, a_other, first)
        first, place_later = lax.optimization_barrier((first, place))
        first = shared(first.reshape(NX, -1, half), "x", 1.0)
        first = shared(first.reshape(NY, -1, half), "y", 0.25)
    with jax.named_scope("second"):
        second_half = terms(False, place_later, g_other, x_other, a_other, second_half)
        second_half = shared(second_half.reshape(NY, -1, half), "y", 1.0)
        second_half = shared(second_half.reshape(NX, -1, half), "x", 0.25)
    with jax.named_scope("depth_sum"):
        part = jnp.concatenate([first, second_half], axis=1) * (4.0 / SEND_SCALE)
        part = part.reshape(NZL, PROJ, width)
        part = part[0] + ahead(part[1], 1) + ahead(part[3], 7) + ahead(part[2], 2)
        gradient = part + lax.ppermute(part, "zh", swap)
    with jax.named_scope("own_row"):
        row = lax.axis_index("y") * NX + lax.axis_index("x")

        def piece(a):
            return lax.dynamic_slice(a, (row, 0), (1, PROJ * width)).reshape(PROJ, width)

        stepped, _, _ = adam_update(gradient, piece(master), piece(moment), piece(second))
        scale = jnp.sqrt(jnp.sum(stepped * stepped, axis=1, keepdims=True) + 1e-06)
        unit = lax.reduce_precision(stepped / scale, 8, 7)
        unit = (unit * UNIT_SCALE).astype(jnp.float16)
        coarse = lax.reduce_precision(gradient, 8, 7)
        fine = (gradient - coarse).astype(jnp.float16)
        coarse = coarse.astype(jnp.float16)
    with jax.named_scope("depth_gather"):
        units = lax.all_to_all(
            jnp.broadcast_to(unit[None], (NZL, PROJ, width)), "zl", 0, 0, tiled=True
        )
    with jax.named_scope("plane_gather"):
        payload = jnp.concatenate([units.reshape(NZL * PROJ, width), coarse, fine], axis=0)
        own = lax.all_gather(payload, ("y", "x"), axis=0, tiled=True).astype(jnp.bfloat16)
        own = own.reshape(PLANE, 24, width)
        grads = own[:, NZL * PROJ :].reshape(2 * PLANE * PROJ, width)
        own = own[:, : NZL * PROJ].reshape(PLANE * NZL * PROJ, width)
    other = lax.ppermute(own, "c", swap)
    new_master, new_moment, new_second = step(grads, master, moment, second)
    gathered = lay(place, own, other, NZL * NC * master.shape[0])
    return (new_master, new_moment, new_second, gathered)


def solution(mesh):
    fine = Mesh(mesh.devices.reshape(NY, NX, NZH, NZL, NC), REP + SHARD)
    tokens = P(REP + SHARD, None)
    rows = P(SHARD, None)
    return jax.shard_map(
        shards,
        mesh=fine,
        in_specs=(tokens, tokens, tokens, rows, rows, rows),
        out_specs=(rows, rows, rows, P()),
        check_vma=False,
    )
```

```python
import functools

import jax
import jax.numpy as jnp
from jax import lax
from jax.experimental import pallas as pl
from jax.experimental.pallas import tpu as pltpu
from jax.sharding import Mesh
from jax.sharding import PartitionSpec as P

beta_one = 0.9
beta_two = 0.95
learn_rate = 0.002
bias_one = 1.0 - 0.9**10
bias_two = 1.0 - 0.95**10

REP = ("y", "x", "zh")
SHARD = ("zl", "c")
NY, NX, NZH, NZL, NC = 4, 4, 2, 4, 2
PLANE = NY * NX
PROJ = 4
SEND_SCALE = 128.0
UNIT_SCALE = 32768.0


def adam_update(gradient, master, moment, second):
    new_moment = beta_one * moment + (1.0 - beta_one) * gradient
    new_second = beta_two * second + (1.0 - beta_two) * gradient * gradient
    stepped = master - learn_rate * (new_moment / bias_one) / (
        jnp.sqrt(new_second / bias_two) + 1e-08
    )
    return (stepped, new_moment, new_second)


def lefts_kernel(place_ref, g_ref, own_ref, send_ref):
    shape = (own_ref.shape[0], g_ref.shape[1])
    m = lax.broadcasted_iota(jnp.int32, shape, 0)
    j = lax.broadcasted_iota(jnp.int32, shape, 1)
    core, depth, x, y = (place_ref[n] for n in range(4))
    first, second = m >> 7, (m >> 5) & 3
    start = 128 * ((depth + (m >> 3)) & 3) + 64 * ((m >> 2) & 1) + (m & 3)
    for out_ref, order in ((own_ref, core), (send_ref, 1 - core)):
        turn = order * (second - first)
        i = 4 * ((y + second - turn) & 3) + ((x + first + turn) & 3)
        chosen = jnp.where(j == start + 4 * i, 1.0, 0.0).astype(jnp.bfloat16)
        out_ref[...] = lax.dot_general(
            chosen, g_ref[...], (((1,), (1,)), ((), ())), preferred_element_type=jnp.float32
        ).astype(jnp.bfloat16)


def lefts(place, g):
    shape = jax.ShapeDtypeStruct((g.shape[1], g.shape[0]), g.dtype)
    return pl.pallas_call(
        lefts_kernel,
        in_specs=[pl.BlockSpec(memory_space=pltpu.SMEM), pl.BlockSpec(memory_space=pltpu.VMEM)],
        out_specs=[pl.BlockSpec(memory_space=pltpu.VMEM)] * 2,
        out_shape=[shape] * 2,
        compiler_params=pltpu.CompilerParams(vmem_limit_bytes=16 * 2**20),
        cost_estimate=pl.CostEstimate(flops=4 * g.size * g.shape[1], bytes_accessed=6 * g.size, transcendentals=0),
        name="lefts",
    )(place, g)


def mask_rows(left_ref, rows, masked_ref):
    left = left_ref[rows]
    k = lax.broadcasted_iota(jnp.int32, left.shape, 0) & 3
    masked_ref[0] = jnp.where(k < 3, left.astype(jnp.float32), 0.0).astype(left.dtype)
    masked_ref[1] = jnp.where(k == 3, left.astype(jnp.float32), 0.0).astype(left.dtype)


def two_dots(left_ref, x_ref, a_ref):
    total = jnp.dot(left_ref[0], x_ref[...], preferred_element_type=jnp.float32)
    return total + jnp.dot(left_ref[1], a_ref[...], preferred_element_type=jnp.float32)


def terms_kernel(rows, sides, *refs):
    inputs, (base_refs, out_ref, masked) = refs[: 3 * sides], (refs[3 * sides : -1 - sides], refs[-1 - sides], refs[-sides:])
    groups = [inputs[3 * n : 3 * n + 3] for n in range(sides)]

    @pl.when(pl.program_id(0) == 0)
    def _():
        for (left_ref, _, _), masked_ref in zip(groups, masked):
            mask_rows(left_ref, rows, masked_ref)

    total = base_refs[0][...] if base_refs else 0.0
    for (_, x_ref, a_ref), masked_ref in zip(groups, masked):
        total += two_dots(masked_ref, x_ref, a_ref)
    out_ref[...] = total


def terms(rows, *sides, base=None, tile=512):
    tokens, width = sides[0][1].shape
    count = rows.stop - rows.start
    left = pl.BlockSpec(sides[0][0].shape, lambda j: (0, 0))
    block = pl.BlockSpec((tokens, tile), lambda j: (0, j))
    result = pl.BlockSpec((count, tile), lambda j: (0, j))
    bases = [] if base is None else [base]
    return pl.pallas_call(
        functools.partial(terms_kernel, rows, len(sides)),
        grid=(width // tile,),
        in_specs=[left, block, block] * len(sides) + [result] * len(bases),
        out_specs=result,
        out_shape=jax.ShapeDtypeStruct((count, width), jnp.float32),
        scratch_shapes=[pltpu.VMEM((2, count, tokens), jnp.bfloat16)] * len(sides),
        compiler_params=pltpu.CompilerParams(vmem_limit_bytes=24 * 2**20),
        cost_estimate=pl.CostEstimate(
            flops=4 * len(sides) * count * tokens * width,
            bytes_accessed=8 * tokens * width,
            transcendentals=0,
        ),
        name="terms",
    )(*(a for side in sides for a in side), *bases)


def step_kernel(g_ref, master_ref, moment_ref, second_ref, nm_ref, mo_ref, se_ref, grad_ref):
    k = pl.program_id(0)
    rows, width = master_ref.shape

    @pl.when(k == 0)
    def _():
        shape = (PROJ * rows, g_ref.shape[0])
        m = lax.broadcasted_iota(jnp.int32, shape, 0)
        j = lax.broadcasted_iota(jnp.int32, shape, 1)
        coarse = g_ref[...].astype(jnp.bfloat16)
        fine = (g_ref[...] - coarse.astype(jnp.float32)).astype(jnp.bfloat16)
        for at in range(2):
            wanted = j == 2 * PROJ * (m & 15) + PROJ * at + (m >> 4)
            pick = jnp.where(wanted, 1.0, 0.0).astype(jnp.bfloat16)
            total = jnp.dot(pick, coarse, preferred_element_type=jnp.float32)
            total += jnp.dot(pick, fine, preferred_element_type=jnp.float32)
            grad_ref[:, at * width // 2 : (at + 1) * width // 2] = total

    gradient = grad_ref[pl.ds(pl.multiple_of(k * rows, rows), rows), :]
    stepped, new_moment, new_second = adam_update(
        gradient, master_ref[...], moment_ref[...], second_ref[...]
    )
    mo_ref[...] = new_moment
    se_ref[...] = new_second
    scale = jnp.sqrt(jnp.sum(stepped * stepped, axis=1, keepdims=True) + 1e-06)
    nm_ref[...] = stepped / scale


def step(u, master, moment, second):
    rows, width = master.shape
    width //= PROJ
    block = pl.BlockSpec((rows, width), lambda k: (0, k))
    return pl.pallas_call(
        step_kernel,
        grid=(PROJ,),
        in_specs=[pl.BlockSpec(u.shape, lambda k: (0, 0)), block, block, block],
        out_specs=[block, block, block],
        out_shape=[jax.ShapeDtypeStruct(master.shape, jnp.float32)] * 3,
        scratch_shapes=[pltpu.VMEM((PROJ * rows, width), jnp.float32)],
        compiler_params=pltpu.CompilerParams(vmem_limit_bytes=40 * 2**20),
        cost_estimate=pl.CostEstimate(
            flops=2 * 64 * 128 * width, bytes_accessed=24 * rows * width * PROJ, transcendentals=0
        ),
        name="step",
    )(u, master, moment, second)


def lay_kernel(place_ref, own_ref, other_ref, out_ref, held_ref, sems):
    j = pl.program_id(0)
    last = pl.num_programs(0) - 1
    parts, tile = own_ref.shape
    width = tile * (last + 1)
    slot = lax.rem(j, 2)

    def copies(step, slot):
        for k in range(PROJ):
            at = pl.ds(pl.multiple_of(k * width + step * tile, 128), tile)
            yield pltpu.make_async_copy(held_ref.at[slot, k], out_ref.at[:, at], sems.at[slot, k])

    @pl.when(j >= 2)
    def _():
        for copy in copies(j - 2, slot):
            copy.wait()

    m = lax.broadcasted_iota(jnp.int32, (256, parts), 0)
    n = lax.broadcasted_iota(jnp.int32, (256, parts), 1)
    wanted = n == (m & 15) * 16 + ((m >> 4) & 3) * 4 + (m >> 6)
    pick = jnp.where(wanted, 1.0 / UNIT_SCALE, 0.0).astype(jnp.bfloat16)
    for ref, core in ((own_ref, place_ref[0]), (other_ref, 1 - place_ref[0])):
        rows = jnp.dot(pick, ref[...], preferred_element_type=jnp.float32).astype(out_ref.dtype)
        for k in range(PROJ):
            for zl in range(NZL):
                to = pl.ds(pl.multiple_of(32 * zl + 16 * core, 16), 16)
                held_ref[slot, k, to] = rows[64 * k + 16 * zl : 64 * k + 16 * zl + 16]
    for copy in copies(j, slot):
        copy.start()

    @pl.when(j == last)
    def _():
        for copy in copies(j - 1, 1 - slot):
            copy.wait()
        for copy in copies(j, slot):
            copy.wait()


def lay(place, own, other, rows, tile=1536):
    parts, half = own.shape[0] // 2, own.shape[1]
    width = 2 * half
    block = pl.BlockSpec((parts, tile), lambda j: (j // (half // tile), j % (half // tile)))
    return pl.pallas_call(
        lay_kernel,
        grid=(width // tile,),
        in_specs=[pl.BlockSpec(memory_space=pltpu.SMEM), block, block],
        out_specs=pl.BlockSpec(memory_space=pl.ANY),
        out_shape=jax.ShapeDtypeStruct((rows, PROJ * width), jnp.bfloat16),
        scratch_shapes=[
            pltpu.VMEM((2, PROJ, rows, tile), jnp.bfloat16),
            pltpu.SemaphoreType.DMA((2, PROJ)),
        ],
        compiler_params=pltpu.CompilerParams(vmem_limit_bytes=24 * 2**20),
        cost_estimate=pl.CostEstimate(
            flops=4 * 256 * parts * width, bytes_accessed=8 * parts * width, transcendentals=0
        ),
        name="lay",
    )(place, own, other)


def shards(x_in, attn_out, grads_out, master, moment, second):
    width = x_in.shape[1]
    swap = [(0, 1), (1, 0)]
    core = lax.axis_index("c")
    place = jnp.stack([lax.axis_index(name) for name in ("c", "zl", "x", "y")]).astype(jnp.int32)
    half = width // 2

    def ahead(a, by):
        ring = NZH * NZL
        return lax.ppermute(a, ("zh", "zl"), [(z, (z + by) % ring) for z in range(ring)])

    def onward(a, by, turned):
        pairs = []
        for n in range(PLANE * NC):
            y, x, core = n // (NX * NC), n // NC % NX, n % NC
            to_y, to_x = ((y + by) % NY, x) if core != turned else (y, (x + by) % NX)
            pairs.append((n, (to_y * NX + to_x) * NC + core))
        return lax.ppermute(a, ("y", "x", "c"), pairs)

    def shared(kept, rows, turned):
        blocks = rows.astype(jnp.float16).reshape(3, -1, half)
        came = [onward(blocks[n - 1], n, turned).astype(jnp.float32) for n in (1, 3, 2)]
        return kept + came[0] + came[1] + came[2]

    def columns(a, which):
        return lax.dynamic_slice_in_dim(a, which * half, half, axis=1)

    with jax.named_scope("pair"):
        left, left_send = lefts(place, grads_out)
        left_other = lax.ppermute(left_send, "c", swap)
        x_other = lax.ppermute(columns(x_in, 1 - core), "c", swap)
        a_other = lax.ppermute(columns(attn_out, 1 - core), "c", swap)
        own = (left, columns(x_in, core), columns(attn_out, core))
        other = (left_other, x_other, a_other)
        block = grads_out.shape[1] // 4
        going, staying = slice(block, 4 * block), slice(0, block)
        sent = terms(going, other, base=terms(going, own))
    with jax.named_scope("plane_sum"):
        part = shared(terms(staying, own, other) * SEND_SCALE, sent * SEND_SCALE, 0)
        part = part * 0.25
        part = shared(part[: block // 4], part[block // 4 :], 1)
    with jax.named_scope("depth_sum"):
        part = (part * (4.0 / SEND_SCALE)).reshape(NZL, NC * PROJ, half)
        part = part[0] + ahead(part[1], 1) + ahead(part[3], 7) + ahead(part[2], 2)
        part = part + lax.ppermute(part, "zh", swap)
        came = lax.ppermute(part, "c", swap)
        gradient = jnp.where(
            core == 0,
            jnp.concatenate([part[:PROJ], came[:PROJ]], axis=1),
            jnp.concatenate([came[PROJ:], part[PROJ:]], axis=1),
        )
    with jax.named_scope("own_row"):
        row = lax.axis_index("y") * NX + lax.axis_index("x")

        def piece(a):
            return lax.dynamic_slice(a, (row, 0), (1, PROJ * width)).reshape(PROJ, width)

        stepped, _, _ = adam_update(gradient, piece(master), piece(moment), piece(second))
        scale = jnp.sqrt(jnp.sum(stepped * stepped, axis=1, keepdims=True) + 1e-06)
        unit = lax.reduce_precision(stepped / scale, 8, 7)
        unit = (unit * UNIT_SCALE).astype(jnp.float16)
    with jax.named_scope("depth_gather"):
        units = lax.all_to_all(
            jnp.broadcast_to(unit[None], (NZL, PROJ, width)), "zl", 0, 0, tiled=True
        )
    with jax.named_scope("plane_gather"):
        units = units.reshape(NZL * PROJ, width)
        small = gradient.astype(jnp.float16)
        halves = [a[:, n * half : (n + 1) * half] for a in (units, small) for n in range(2)]
        came = lax.all_gather(jnp.concatenate(halves, axis=0), ("y", "x"), axis=0, tiled=True)
        came = came.reshape(PLANE, 2 * (NZL + 1) * PROJ, half)
        grads = came[:, 2 * NZL * PROJ :].astype(jnp.float32).reshape(2 * PLANE * PROJ, half)
        own = came[:, : 2 * NZL * PROJ].astype(jnp.bfloat16)
        own = jnp.swapaxes(own.reshape(PLANE, 2, NZL * PROJ, half), 0, 1)
        own = own.reshape(2 * PLANE * NZL * PROJ, half)
    other = lax.ppermute(own, "c", swap)
    new_master, new_moment, new_second = step(grads, master, moment, second)
    gathered = lay(place, own, other, NZL * NC * master.shape[0])
    return (new_master, new_moment, new_second, gathered)


def solution(mesh):
    fine = Mesh(mesh.devices.reshape(NY, NX, NZH, NZL, NC), REP + SHARD)
    tokens = P(REP + SHARD, None)
    rows = P(SHARD, None)
    return jax.shard_map(
        shards,
        mesh=fine,
        in_specs=(tokens, tokens, tokens, rows, rows, rows),
        out_specs=(rows, rows, rows, P()),
        check_vma=False,
    )
```

```python
import functools

import jax
import jax.numpy as jnp
from jax import lax
from jax.experimental import pallas as pl
from jax.experimental.pallas import tpu as pltpu
from jax.sharding import Mesh
from jax.sharding import PartitionSpec as P

beta_one = 0.9
beta_two = 0.95
learn_rate = 0.002
bias_one = 1.0 - 0.9**10
bias_two = 1.0 - 0.95**10

REP = ("y", "x", "zh")
SHARD = ("zl", "c")
NY, NX, NZH, NZL, NC = 4, 4, 2, 4, 2
PLANE = NY * NX
PROJ = 4
SEND_SCALE = 128.0
UNIT_SCALE = 32768.0


def adam_update(gradient, master, moment, second):
    new_moment = beta_one * moment + (1.0 - beta_one) * gradient
    new_second = beta_two * second + (1.0 - beta_two) * gradient * gradient
    stepped = master - (learn_rate / bias_one) * new_moment / (
        jnp.sqrt(new_second * (1.0 / bias_two)) + 1e-08
    )
    return (stepped, new_moment, new_second)


def lefts_kernel(place_ref, g_ref, own_ref, send_ref):
    shape = (own_ref.shape[0], g_ref.shape[1])
    m = lax.broadcasted_iota(jnp.int32, shape, 0)
    j = lax.broadcasted_iota(jnp.int32, shape, 1)
    core, depth, x, y = (place_ref[n] for n in range(4))
    first, second = m >> 7, (m >> 5) & 3
    start = 128 * ((depth + (m >> 3)) & 3) + 64 * ((m >> 2) & 1) + (m & 3)
    for out_ref, order in ((own_ref, core), (send_ref, 1 - core)):
        turn = order * (second - first)
        i = 4 * ((y + second - turn) & 3) + ((x + first + turn) & 3)
        chosen = jnp.where(j == start + 4 * i, 1.0, 0.0).astype(jnp.bfloat16)
        out_ref[...] = lax.dot_general(
            chosen, g_ref[...], (((1,), (1,)), ((), ())), preferred_element_type=jnp.float32
        ).astype(jnp.bfloat16)


def lefts(place, g):
    shape = jax.ShapeDtypeStruct((g.shape[1], g.shape[0]), g.dtype)
    return pl.pallas_call(
        lefts_kernel,
        in_specs=[pl.BlockSpec(memory_space=pltpu.SMEM), pl.BlockSpec(memory_space=pltpu.VMEM)],
        out_specs=[pl.BlockSpec(memory_space=pltpu.VMEM)] * 2,
        out_shape=[shape] * 2,
        compiler_params=pltpu.CompilerParams(vmem_limit_bytes=16 * 2**20),
        cost_estimate=pl.CostEstimate(flops=4 * g.size * g.shape[1], bytes_accessed=6 * g.size, transcendentals=0),
        name="lefts",
    )(place, g)


def mask_rows(left_ref, rows, masked_ref):
    left = left_ref[rows]
    k = lax.broadcasted_iota(jnp.int32, left.shape, 0) & 3
    masked_ref[0] = jnp.where(k < 3, left.astype(jnp.float32), 0.0).astype(left.dtype)
    masked_ref[1] = jnp.where(k == 3, left.astype(jnp.float32), 0.0).astype(left.dtype)


def terms_kernel(rows, sides, tile, *refs):
    inputs, rest = refs[: 3 * sides], refs[3 * sides :]
    bases, out_ref, masked = rest[: -1 - sides], rest[-1 - sides], rest[-sides:]
    groups = [inputs[3 * n : 3 * n + 3] for n in range(sides)]
    for (left_ref, _, _), masked_ref in zip(groups, masked):
        mask_rows(left_ref, rows, masked_ref)

    @pl.loop(0, out_ref.shape[1] // tile)
    def _(j):
        at = pl.ds(pl.multiple_of(j * tile, tile), tile)
        total = bases[0][:, at] if bases else 0.0
        for (_, x_ref, a_ref), masked_ref in zip(groups, masked):
            total += jnp.dot(masked_ref[0], x_ref[:, at], preferred_element_type=jnp.float32)
            total += jnp.dot(masked_ref[1], a_ref[:, at], preferred_element_type=jnp.float32)
        out_ref[:, at] = total


def terms(rows, *sides, base=None, tile=512):
    tokens, width = sides[0][1].shape
    count = rows.stop - rows.start
    operands = [a for side in sides for a in side] + ([] if base is None else [base])
    return pl.pallas_call(
        functools.partial(terms_kernel, rows, len(sides), tile),
        in_specs=[pl.BlockSpec(memory_space=pltpu.VMEM)] * len(operands),
        out_specs=pl.BlockSpec(memory_space=pltpu.VMEM),
        out_shape=jax.ShapeDtypeStruct((count, width), jnp.float32),
        scratch_shapes=[pltpu.VMEM((2, count, tokens), jnp.bfloat16)] * len(sides),
        compiler_params=pltpu.CompilerParams(vmem_limit_bytes=32 * 2**20),
        cost_estimate=pl.CostEstimate(
            flops=4 * len(sides) * count * tokens * width,
            bytes_accessed=8 * tokens * width,
            transcendentals=0,
        ),
        name="terms",
    )(*operands)


def step_kernel(g_ref, *refs):
    state_refs, out_refs, (made, grad_ref, out_sems) = refs[:3], refs[3:6], refs[6:]
    rows, width = grad_ref.shape[0] // PROJ, grad_ref.shape[1]

    def part(k):
        return slice(None), slice(k * width, (k + 1) * width)

    def leaving(n, k):
        return pltpu.make_async_copy(made.at[n, k], out_refs[n].at[part(k)], out_sems.at[n, k])

    shape = (PROJ * rows, g_ref.shape[0])
    m = lax.broadcasted_iota(jnp.int32, shape, 0)
    j = lax.broadcasted_iota(jnp.int32, shape, 1)
    coarse = g_ref[...].astype(jnp.bfloat16)
    fine = (g_ref[...] - coarse.astype(jnp.float32)).astype(jnp.bfloat16)
    for at in range(2):
        wanted = j == 2 * PROJ * (m & 15) + PROJ * at + (m >> 4)
        pick = jnp.where(wanted, 1.0, 0.0).astype(jnp.bfloat16)
        total = jnp.dot(pick, coarse, preferred_element_type=jnp.float32)
        total += jnp.dot(pick, fine, preferred_element_type=jnp.float32)
        grad_ref[:, at * width // 2 : (at + 1) * width // 2] = total
    for k in range(PROJ):
        gradient = grad_ref[k * rows : (k + 1) * rows]
        stepped, new_moment, new_second = adam_update(
            gradient, *(ref[part(k)] for ref in state_refs)
        )
        made[1, k] = new_moment
        leaving(1, k).start()
        made[2, k] = new_second
        leaving(2, k).start()
        scale = jnp.sqrt(jnp.sum(stepped * stepped, axis=1, keepdims=True) + 1e-06)
        made[0, k] = stepped * (1.0 / scale)
        leaving(0, k).start()
    for k in range(PROJ):
        for n in range(3):
            leaving(n, k).wait()


def step(g, master, moment, second):
    rows, width = master.shape
    width //= PROJ
    anywhere = pl.BlockSpec(memory_space=pl.ANY)
    return pl.pallas_call(
        step_kernel,
        in_specs=[pl.BlockSpec(memory_space=pltpu.VMEM)] * 4,
        out_specs=[anywhere] * 3,
        out_shape=[jax.ShapeDtypeStruct(master.shape, jnp.float32)] * 3,
        scratch_shapes=[
            pltpu.VMEM((3, PROJ, rows, width), jnp.float32),
            pltpu.VMEM((PROJ * rows, width), jnp.float32),
            pltpu.SemaphoreType.DMA((3, PROJ)),
        ],
        compiler_params=pltpu.CompilerParams(vmem_limit_bytes=28 * 2**20),
        cost_estimate=pl.CostEstimate(
            flops=20 * 64 * width, bytes_accessed=24 * rows * width * PROJ, transcendentals=0
        ),
        name="step",
    )(g, master, moment, second)


def lay_kernel(place_ref, own_ref, other_ref, out_ref, held_ref, sems):
    slots, tile = sems.shape[0], held_ref.shape[3]
    parts, half = own_ref.shape[0] // 2, own_ref.shape[1]
    m = lax.broadcasted_iota(jnp.int32, (parts, parts), 0)
    n = lax.broadcasted_iota(jnp.int32, (parts, parts), 1)
    wanted = n == (m & 15) * 16 + ((m >> 4) & 3) * 4 + (m >> 6)
    pick = jnp.where(wanted, 1.0 / UNIT_SCALE, 0.0).astype(jnp.bfloat16)

    def leaving(j, k):
        at = slice(k * 2 * half + j * tile, k * 2 * half + (j + 1) * tile)
        return pltpu.make_async_copy(
            held_ref.at[j % slots, k], out_ref.at[:, at], sems.at[j % slots, k]
        )

    steps = 2 * half // tile
    for j in range(steps):
        if j >= slots:
            for k in range(PROJ):
                leaving(j - slots, k).wait()
        side, at = divmod(j * tile, half)
        for ref, core in ((own_ref, place_ref[0]), (other_ref, 1 - place_ref[0])):
            values = ref[side * parts : (side + 1) * parts, at : at + tile]
            rows = jnp.dot(pick, values, preferred_element_type=jnp.float32).astype(out_ref.dtype)
            for k in range(PROJ):
                for zl in range(NZL):
                    to = pl.ds(pl.multiple_of(32 * zl + 16 * core, 16), 16)
                    start = 64 * k + 16 * zl
                    held_ref[j % slots, k, to] = rows[start : start + 16]
        for k in range(PROJ):
            leaving(j, k).start()
    for j in range(max(steps - slots, 0), steps):
        for k in range(PROJ):
            leaving(j, k).wait()


def lay(place, own, other, rows, tile=768, slots=4):
    width = 2 * own.shape[1]
    return pl.pallas_call(
        lay_kernel,
        in_specs=[pl.BlockSpec(memory_space=pltpu.SMEM)]
        + [pl.BlockSpec(memory_space=pltpu.VMEM)] * 2,
        out_specs=pl.BlockSpec(memory_space=pl.ANY),
        out_shape=jax.ShapeDtypeStruct((rows, PROJ * width), jnp.bfloat16),
        scratch_shapes=[
            pltpu.VMEM((slots, PROJ, rows, tile), jnp.bfloat16),
            pltpu.SemaphoreType.DMA((slots, PROJ)),
        ],
        compiler_params=pltpu.CompilerParams(vmem_limit_bytes=28 * 2**20),
        cost_estimate=pl.CostEstimate(
            flops=2 * 256 * own.size, bytes_accessed=4 * own.size, transcendentals=0
        ),
        name="lay",
    )(place, own, other)


def shards(x_in, attn_out, grads_out, master, moment, second):
    width = x_in.shape[1]
    swap = [(0, 1), (1, 0)]
    core = lax.axis_index("c")
    place = jnp.stack([lax.axis_index(name) for name in ("c", "zl", "x", "y")]).astype(jnp.int32)
    half = width // 2

    def ahead(a, by):
        ring = NZH * NZL
        return lax.ppermute(a, ("zh", "zl"), [(z, (z + by) % ring) for z in range(ring)])

    def onward(a, by, turned):
        pairs = []
        for n in range(PLANE * NC):
            y, x, core = n // (NX * NC), n // NC % NX, n % NC
            to_y, to_x = ((y + by) % NY, x) if core != turned else (y, (x + by) % NX)
            pairs.append((n, (to_y * NX + to_x) * NC + core))
        return lax.ppermute(a, ("y", "x", "c"), pairs)

    def shared(kept, rows, turned):
        blocks = rows.astype(jnp.float16).reshape(3, -1, half)
        came = [onward(blocks[n - 1], n, turned).astype(jnp.float32) for n in (1, 3, 2)]
        return kept + came[0] + came[1] + came[2]

    def columns(a, which):
        return lax.dynamic_slice_in_dim(a, which * half, half, axis=1)

    with jax.named_scope("pair"):
        left, left_send = lefts(place, grads_out)
        left_other = lax.ppermute(left_send, "c", swap)
        x_other = lax.ppermute(columns(x_in, 1 - core), "c", swap)
        a_other = lax.ppermute(columns(attn_out, 1 - core), "c", swap)
        own = (left, columns(x_in, core), columns(attn_out, core))
        other = (left_other, x_other, a_other)
        block = grads_out.shape[1] // 4
        going, staying = slice(block, 4 * block), slice(0, block)
        sent = terms(going, other, base=terms(going, own))
    with jax.named_scope("plane_sum"):
        part = shared(terms(staying, own, other) * SEND_SCALE, sent * SEND_SCALE, 0)
        part = part * 0.25
        part = shared(part[: block // 4], part[block // 4 :], 1)
    with jax.named_scope("depth_sum"):
        part = (part * (4.0 / SEND_SCALE)).reshape(NZL, NC * PROJ, half)
        part = part[0] + ahead(part[1], 1) + ahead(part[3], 7) + ahead(part[2], 2)
        part = part + lax.ppermute(part, "zh", swap)
        came = lax.ppermute(part, "c", swap)
        gradient = jnp.where(
            core == 0,
            jnp.concatenate([part[:PROJ], came[:PROJ]], axis=1),
            jnp.concatenate([came[PROJ:], part[PROJ:]], axis=1),
        )
    with jax.named_scope("own_row"):
        row = lax.axis_index("y") * NX + lax.axis_index("x")

        def piece(a):
            return lax.dynamic_slice(a, (row, 0), (1, PROJ * width)).reshape(PROJ, width)

        stepped, _, _ = adam_update(gradient, piece(master), piece(moment), piece(second))
        scale = jnp.sqrt(jnp.sum(stepped * stepped, axis=1, keepdims=True) + 1e-06)
        unit = lax.reduce_precision(stepped / scale, 8, 7)
        unit = (unit * UNIT_SCALE).astype(jnp.float16)
    with jax.named_scope("depth_gather"):
        units = lax.all_to_all(
            jnp.broadcast_to(unit[None], (NZL, PROJ, width)), "zl", 0, 0, tiled=True
        )
    with jax.named_scope("plane_gather"):
        units = units.reshape(NZL * PROJ, width)
        small = gradient.astype(jnp.float16)
        halves = [a[:, n * half : (n + 1) * half] for a in (units, small) for n in range(2)]
        came = lax.all_gather(jnp.concatenate(halves, axis=0), ("y", "x"), axis=0, tiled=True)
        came = came.reshape(PLANE, 2 * (NZL + 1) * PROJ, half)
        grads = came[:, 2 * NZL * PROJ :].astype(jnp.float32).reshape(2 * PLANE * PROJ, half)
        own = came[:, : 2 * NZL * PROJ].astype(jnp.bfloat16)
        own = jnp.swapaxes(own.reshape(PLANE, 2, NZL * PROJ, half), 0, 1)
        own = own.reshape(2 * PLANE * NZL * PROJ, half)
    other = lax.ppermute(own, "c", swap)
    new_master, new_moment, new_second = step(grads, master, moment, second)
    gathered = lay(place, own, other, NZL * NC * master.shape[0])
    return (new_master, new_moment, new_second, gathered)


def solution(mesh):
    fine = Mesh(mesh.devices.reshape(NY, NX, NZH, NZL, NC), REP + SHARD)
    tokens = P(REP + SHARD, None)
    rows = P(SHARD, None)
    return jax.shard_map(
        shards,
        mesh=fine,
        in_specs=(tokens, tokens, tokens, rows, rows, rows),
        out_specs=(rows, rows, rows, P()),
        check_vma=False,
    )
```

```python
import functools

import jax
import jax.numpy as jnp
import numpy as np
from jax import lax
from jax.experimental import pallas as pl
from jax.experimental.pallas import tpu as pltpu
from jax.sharding import Mesh
from jax.sharding import PartitionSpec as P

beta_one = 0.9
beta_two = 0.95
learn_rate = 0.002
bias_one = 1.0 - 0.9**10
bias_two = 1.0 - 0.95**10

REP = ("y", "x", "zh")
SHARD = ("zl", "c")
NY, NX, NZH, NZL, NC = 4, 4, 2, 4, 2
PLANE = NY * NX
PROJ = 4
SEND_SCALE = 128.0
UNIT_SCALE = 32768.0


def adam_update(gradient, master, moment, second):
    new_moment = beta_one * moment + (1.0 - beta_one) * gradient
    new_second = beta_two * second + (1.0 - beta_two) * gradient * gradient
    stepped = master - (learn_rate / bias_one) * new_moment / (
        jnp.sqrt(new_second * (1.0 / bias_two)) + 1e-08
    )
    return (stepped, new_moment, new_second)


def lefts_kernel(place_ref, g_ref, own_ref, send_ref):
    shape = (own_ref.shape[0], g_ref.shape[1])
    m = lax.broadcasted_iota(jnp.int32, shape, 0)
    j = lax.broadcasted_iota(jnp.int32, shape, 1)
    core, depth, x, y = (place_ref[n] for n in range(4))
    first, second = m >> 7, (m >> 5) & 3
    start = 128 * ((depth + (m >> 3)) & 3) + 64 * ((m >> 2) & 1) + (m & 3)
    for out_ref, order in ((own_ref, core), (send_ref, 1 - core)):
        turn = order * (second - first)
        i = 4 * ((y + second - turn) & 3) + ((x + first + turn) & 3)
        chosen = jnp.where(j == start + 4 * i, 1.0, 0.0).astype(jnp.bfloat16)
        out_ref[...] = lax.dot_general(
            chosen, g_ref[...], (((1,), (1,)), ((), ())), preferred_element_type=jnp.float32
        ).astype(jnp.bfloat16)


def lefts(place, g):
    shape = jax.ShapeDtypeStruct((g.shape[1], g.shape[0]), g.dtype)
    return pl.pallas_call(
        lefts_kernel,
        in_specs=[pl.BlockSpec(memory_space=pltpu.SMEM), pl.BlockSpec(memory_space=pltpu.VMEM)],
        out_specs=[pl.BlockSpec(memory_space=pltpu.VMEM)] * 2,
        out_shape=[shape] * 2,
        compiler_params=pltpu.CompilerParams(vmem_limit_bytes=16 * 2**20),
        cost_estimate=pl.CostEstimate(flops=4 * g.size * g.shape[1], bytes_accessed=6 * g.size, transcendentals=0),
        name="lefts",
    )(place, g)


def mask_rows(left_ref, rows, masked_ref):
    left = left_ref[rows]
    k = lax.broadcasted_iota(jnp.int32, left.shape, 0) & 3
    masked_ref[0] = jnp.where(k < 3, left.astype(jnp.float32), 0.0).astype(left.dtype)
    masked_ref[1] = jnp.where(k == 3, left.astype(jnp.float32), 0.0).astype(left.dtype)


def terms_kernel(rows, sides, tile, *refs):
    inputs, rest = refs[: 3 * sides], refs[3 * sides :]
    bases, out_ref, masked = rest[: -1 - sides], rest[-1 - sides], rest[-sides:]
    groups = [inputs[3 * n : 3 * n + 3] for n in range(sides)]
    for (left_ref, _, _), masked_ref in zip(groups, masked):
        mask_rows(left_ref, rows, masked_ref)

    @pl.loop(0, out_ref.shape[1] // tile)
    def _(j):
        at = pl.ds(pl.multiple_of(j * tile, tile), tile)
        total = bases[0][:, at] if bases else 0.0
        for (_, x_ref, a_ref), masked_ref in zip(groups, masked):
            total += jnp.dot(masked_ref[0], x_ref[:, at], preferred_element_type=jnp.float32)
            total += jnp.dot(masked_ref[1], a_ref[:, at], preferred_element_type=jnp.float32)
        out_ref[:, at] = total


def terms(rows, *sides, base=None, tile=512):
    tokens, width = sides[0][1].shape
    count = rows.stop - rows.start
    operands = [a for side in sides for a in side] + ([] if base is None else [base])
    return pl.pallas_call(
        functools.partial(terms_kernel, rows, len(sides), tile),
        in_specs=[pl.BlockSpec(memory_space=pltpu.VMEM)] * len(operands),
        out_specs=pl.BlockSpec(memory_space=pltpu.VMEM),
        out_shape=jax.ShapeDtypeStruct((count, width), jnp.float32),
        scratch_shapes=[pltpu.VMEM((2, count, tokens), jnp.bfloat16)] * len(sides),
        compiler_params=pltpu.CompilerParams(vmem_limit_bytes=32 * 2**20),
        cost_estimate=pl.CostEstimate(
            flops=4 * len(sides) * count * tokens * width,
            bytes_accessed=8 * tokens * width,
            transcendentals=0,
        ),
        name="terms",
    )(*operands)


def step_kernel(g_ref, *refs):
    state_refs, out_refs, (made, grad_ref, out_sems) = refs[:3], refs[3:6], refs[6:]
    rows, width = grad_ref.shape[0] // PROJ, grad_ref.shape[1]

    def part(k):
        return slice(None), slice(k * width, (k + 1) * width)

    def leaving(n, k):
        return pltpu.make_async_copy(made.at[n, k], out_refs[n].at[part(k)], out_sems.at[n, k])

    shape = (PROJ * rows, g_ref.shape[0])
    m = lax.broadcasted_iota(jnp.int32, shape, 0)
    j = lax.broadcasted_iota(jnp.int32, shape, 1)
    coarse = g_ref[...].astype(jnp.bfloat16)
    fine = (g_ref[...] - coarse.astype(jnp.float32)).astype(jnp.bfloat16)
    for at in range(2):
        wanted = j == 2 * PROJ * (m & 15) + PROJ * at + (m >> 4)
        pick = jnp.where(wanted, 1.0, 0.0).astype(jnp.bfloat16)
        total = jnp.dot(pick, coarse, preferred_element_type=jnp.float32)
        total += jnp.dot(pick, fine, preferred_element_type=jnp.float32)
        grad_ref[:, at * width // 2 : (at + 1) * width // 2] = total
    for k in range(PROJ):
        gradient = grad_ref[k * rows : (k + 1) * rows]
        stepped, new_moment, new_second = adam_update(
            gradient, *(ref[part(k)] for ref in state_refs)
        )
        made[1, k] = new_moment
        leaving(1, k).start()
        made[2, k] = new_second
        leaving(2, k).start()
        scale = jnp.sqrt(jnp.sum(stepped * stepped, axis=1, keepdims=True) + 1e-06)
        made[0, k] = stepped * (1.0 / scale)
        leaving(0, k).start()
    for k in range(PROJ):
        for n in range(3):
            leaving(n, k).wait()


def step(g, master, moment, second):
    rows, width = master.shape
    width //= PROJ
    anywhere = pl.BlockSpec(memory_space=pl.ANY)
    return pl.pallas_call(
        step_kernel,
        in_specs=[pl.BlockSpec(memory_space=pltpu.VMEM)] * 4,
        out_specs=[anywhere] * 3,
        out_shape=[jax.ShapeDtypeStruct(master.shape, jnp.float32)] * 3,
        scratch_shapes=[
            pltpu.VMEM((3, PROJ, rows, width), jnp.float32),
            pltpu.VMEM((PROJ * rows, width), jnp.float32),
            pltpu.SemaphoreType.DMA((3, PROJ)),
        ],
        compiler_params=pltpu.CompilerParams(vmem_limit_bytes=28 * 2**20),
        cost_estimate=pl.CostEstimate(
            flops=20 * 64 * width, bytes_accessed=24 * rows * width * PROJ, transcendentals=0
        ),
        name="step",
    )(g, master, moment, second)


def lay_kernel(place_ref, own_ref, other_ref, out_ref, held_ref, sems):
    slots, tile = sems.shape[0], held_ref.shape[3]
    parts, half = own_ref.shape[0] // 2, own_ref.shape[1]
    m = lax.broadcasted_iota(jnp.int32, (parts, parts), 0)
    n = lax.broadcasted_iota(jnp.int32, (parts, parts), 1)
    ahead = ((m >> 4) - place_ref[1]) & 3
    wanted = n == (m & 15) * 16 + ahead * 4 + (m >> 6)
    pick = jnp.where(wanted, 1.0 / UNIT_SCALE, 0.0).astype(jnp.bfloat16)

    def leaving(j, k):
        at = slice(k * 2 * half + j * tile, k * 2 * half + (j + 1) * tile)
        return pltpu.make_async_copy(
            held_ref.at[j % slots, k], out_ref.at[:, at], sems.at[j % slots, k]
        )

    steps = 2 * half // tile
    for j in range(steps):
        if j >= slots:
            for k in range(PROJ):
                leaving(j - slots, k).wait()
        side, at = divmod(j * tile, half)
        for ref, core in ((own_ref, place_ref[0]), (other_ref, 1 - place_ref[0])):
            values = ref[side * parts : (side + 1) * parts, at : at + tile]
            rows = jnp.dot(pick, values, preferred_element_type=jnp.float32).astype(out_ref.dtype)
            for k in range(PROJ):
                for zl in range(NZL):
                    to = pl.ds(pl.multiple_of(32 * zl + 16 * core, 16), 16)
                    start = 64 * k + 16 * zl
                    held_ref[j % slots, k, to] = rows[start : start + 16]
        for k in range(PROJ):
            leaving(j, k).start()
    for j in range(max(steps - slots, 0), steps):
        for k in range(PROJ):
            leaving(j, k).wait()


def lay(place, own, other, rows, tile=768, slots=4):
    width = 2 * own.shape[1]
    return pl.pallas_call(
        lay_kernel,
        in_specs=[pl.BlockSpec(memory_space=pltpu.SMEM)]
        + [pl.BlockSpec(memory_space=pltpu.VMEM)] * 2,
        out_specs=pl.BlockSpec(memory_space=pl.ANY),
        out_shape=jax.ShapeDtypeStruct((rows, PROJ * width), jnp.bfloat16),
        scratch_shapes=[
            pltpu.VMEM((slots, PROJ, rows, tile), jnp.bfloat16),
            pltpu.SemaphoreType.DMA((slots, PROJ)),
        ],
        compiler_params=pltpu.CompilerParams(vmem_limit_bytes=28 * 2**20),
        cost_estimate=pl.CostEstimate(
            flops=2 * 256 * own.size, bytes_accessed=4 * own.size, transcendentals=0
        ),
        name="lay",
    )(place, own, other)


def shards(x_in, attn_out, grads_out, master, moment, second):
    width = x_in.shape[1]
    swap = [(0, 1), (1, 0)]
    core = lax.axis_index("c")
    place = jnp.stack([lax.axis_index(name) for name in ("c", "zl", "x", "y")]).astype(jnp.int32)
    half = width // 2

    def ahead(a, by):
        ring = NZH * NZL
        return lax.ppermute(a, ("zh", "zl"), [(z, (z + by) % ring) for z in range(ring)])

    def onward(a, by, turned):
        pairs = []
        for n in range(PLANE * NC):
            y, x, core = n // (NX * NC), n // NC % NX, n % NC
            to_y, to_x = ((y + by) % NY, x) if core != turned else (y, (x + by) % NX)
            pairs.append((n, (to_y * NX + to_x) * NC + core))
        return lax.ppermute(a, ("y", "x", "c"), pairs)

    def shared(kept, rows, turned):
        blocks = rows.astype(jnp.float16).reshape(3, -1, half)
        came = [onward(blocks[n - 1], n, turned).astype(jnp.float32) for n in (1, 3, 2)]
        return kept + came[0] + came[1] + came[2]

    def columns(a, which):
        return lax.dynamic_slice_in_dim(a, which * half, half, axis=1)

    with jax.named_scope("pair"):
        left, left_send = lefts(place, grads_out)
        left_other = lax.ppermute(left_send, "c", swap)
        x_other = lax.ppermute(columns(x_in, 1 - core), "c", swap)
        a_other = lax.ppermute(columns(attn_out, 1 - core), "c", swap)
        own = (left, columns(x_in, core), columns(attn_out, core))
        other = (left_other, x_other, a_other)
        block = grads_out.shape[1] // 4
        going, staying = slice(block, 4 * block), slice(0, block)
        sent = terms(going, other, base=terms(going, own))
    with jax.named_scope("plane_sum"):
        part = shared(terms(staying, own, other) * SEND_SCALE, sent * SEND_SCALE, 0)
        part = part * 0.25
        part = shared(part[: block // 4], part[block // 4 :], 1)
    with jax.named_scope("depth_sum"):
        part = (part * (4.0 / SEND_SCALE)).reshape(NZL, NC * PROJ, half)
        part = part[0] + ahead(part[1], 1) + ahead(part[3], 7) + ahead(part[2], 2)
        part = part + lax.ppermute(part, "zh", swap)
        came = lax.ppermute(part, "c", swap)
        gradient = jnp.where(
            core == 0,
            jnp.concatenate([part[:PROJ], came[:PROJ]], axis=1),
            jnp.concatenate([came[PROJ:], part[PROJ:]], axis=1),
        )
    with jax.named_scope("own_row"):
        row = lax.axis_index("y") * NX + lax.axis_index("x")

        def piece(a):
            return lax.dynamic_slice(a, (row, 0), (1, PROJ * width)).reshape(PROJ, width)

        stepped, _, _ = adam_update(gradient, piece(master), piece(moment), piece(second))
        scale = jnp.sqrt(jnp.sum(stepped * stepped, axis=1, keepdims=True) + 1e-06)
        unit = (stepped / scale).astype(jnp.bfloat16)
        unit, small = (
            jnp.concatenate([a[:, :half], a[:, half:]], axis=0) for a in (unit, gradient)
        )
    with jax.named_scope("depth_gather"):
        units = [unit, ahead(unit, 7), ahead(unit, 2), ahead(unit, 1)]
    with jax.named_scope("plane_gather"):
        order = np.arange(2 * NZL * PROJ).reshape(NZL, 2, PROJ).swapaxes(0, 1).reshape(-1)
        turn = jnp.asarray(np.eye(2 * NZL * PROJ)[order] * UNIT_SCALE, jnp.bfloat16)
        units = jnp.dot(turn, jnp.concatenate(units, axis=0), preferred_element_type=jnp.float32)
        payload = jnp.concatenate([units, small], axis=0).astype(jnp.float16)
        came = lax.all_gather(payload, ("y", "x"), axis=0, tiled=True)
        came = came.reshape(PLANE, 2 * (NZL + 1) * PROJ, half)
        grads = came[:, 2 * NZL * PROJ :].astype(jnp.float32).reshape(2 * PLANE * PROJ, half)
        own = came[:, : 2 * NZL * PROJ].astype(jnp.bfloat16)
        own = jnp.swapaxes(own.reshape(PLANE, 2, NZL * PROJ, half), 0, 1)
        own = own.reshape(2 * PLANE * NZL * PROJ, half)
    other = lax.ppermute(own, "c", swap)
    new_master, new_moment, new_second = step(grads, master, moment, second)
    gathered = lay(place, own, other, NZL * NC * master.shape[0])
    return (new_master, new_moment, new_second, gathered)


def solution(mesh):
    fine = Mesh(mesh.devices.reshape(NY, NX, NZH, NZL, NC), REP + SHARD)
    tokens = P(REP + SHARD, None)
    rows = P(SHARD, None)
    return jax.shard_map(
        shards,
        mesh=fine,
        in_specs=(tokens, tokens, tokens, rows, rows, rows),
        out_specs=(rows, rows, rows, P()),
        check_vma=False,
    )
```

```python
import functools

import jax
import jax.numpy as jnp
import numpy as np
from jax import lax
from jax.experimental import pallas as pl
from jax.experimental.pallas import tpu as pltpu
from jax.sharding import Mesh
from jax.sharding import PartitionSpec as P

beta_one = 0.9
beta_two = 0.95
learn_rate = 0.002
bias_one = 1.0 - 0.9**10
bias_two = 1.0 - 0.95**10

REP = ("y", "x", "zh")
SHARD = ("zl", "c")
NY, NX, NZH, NZL, NC = 4, 4, 2, 4, 2
PLANE = NY * NX
PROJ = 4
SEND_SCALE = 128.0
UNIT_SCALE = 32768.0


def adam_update(gradient, master, moment, second):
    new_moment = beta_one * moment + (1.0 - beta_one) * gradient
    new_second = beta_two * second + (1.0 - beta_two) * gradient * gradient
    stepped = master - (learn_rate / bias_one) * new_moment / (
        jnp.sqrt(new_second * (1.0 / bias_two)) + 1e-08
    )
    return (stepped, new_moment, new_second)


def lefts_kernel(place_ref, g_ref, own_ref, send_ref):
    shape = (own_ref.shape[0], g_ref.shape[1])
    m = lax.broadcasted_iota(jnp.int32, shape, 0)
    j = lax.broadcasted_iota(jnp.int32, shape, 1)
    core, depth, x, y = (place_ref[n] for n in range(4))
    first, second = m >> 7, (m >> 5) & 3
    start = 128 * ((depth + (m >> 3)) & 3) + 64 * ((m >> 2) & 1) + (m & 3)
    for out_ref, order in ((own_ref, core), (send_ref, 1 - core)):
        turn = order * (second - first)
        i = 4 * ((y + second - turn) & 3) + ((x + first + turn) & 3)
        chosen = jnp.where(j == start + 4 * i, 1.0, 0.0).astype(jnp.bfloat16)
        out_ref[...] = lax.dot_general(
            chosen, g_ref[...], (((1,), (1,)), ((), ())), preferred_element_type=jnp.float32
        ).astype(jnp.bfloat16)


def lefts(place, g):
    shape = jax.ShapeDtypeStruct((g.shape[1], g.shape[0]), g.dtype)
    return pl.pallas_call(
        lefts_kernel,
        in_specs=[pl.BlockSpec(memory_space=pltpu.SMEM), pl.BlockSpec(memory_space=pltpu.VMEM)],
        out_specs=[pl.BlockSpec(memory_space=pltpu.VMEM)] * 2,
        out_shape=[shape] * 2,
        compiler_params=pltpu.CompilerParams(vmem_limit_bytes=16 * 2**20),
        cost_estimate=pl.CostEstimate(flops=4 * g.size * g.shape[1], bytes_accessed=6 * g.size, transcendentals=0),
        name="lefts",
    )(place, g)


def mask_rows(left_ref, rows, masked_ref):
    left = left_ref[rows]
    k = lax.broadcasted_iota(jnp.int32, left.shape, 0) & 3
    masked_ref[0] = jnp.where(k < 3, left.astype(jnp.float32), 0.0).astype(left.dtype)
    masked_ref[1] = jnp.where(k == 3, left.astype(jnp.float32), 0.0).astype(left.dtype)


def terms_kernel(rows, sides, tile, *refs):
    inputs, rest = refs[: 3 * sides], refs[3 * sides :]
    bases, out_ref, masked = rest[: -1 - sides], rest[-1 - sides], rest[-sides:]
    groups = [inputs[3 * n : 3 * n + 3] for n in range(sides)]
    for (left_ref, _, _), masked_ref in zip(groups, masked):
        mask_rows(left_ref, rows, masked_ref)

    @pl.loop(0, out_ref.shape[1] // tile)
    def _(j):
        at = pl.ds(pl.multiple_of(j * tile, tile), tile)
        total = bases[0][:, at] if bases else 0.0
        for (_, x_ref, a_ref), masked_ref in zip(groups, masked):
            total += jnp.dot(masked_ref[0], x_ref[:, at], preferred_element_type=jnp.float32)
            total += jnp.dot(masked_ref[1], a_ref[:, at], preferred_element_type=jnp.float32)
        out_ref[:, at] = total


def terms(rows, *sides, base=None, tile=512):
    tokens, width = sides[0][1].shape
    count = rows.stop - rows.start
    operands = [a for side in sides for a in side] + ([] if base is None else [base])
    return pl.pallas_call(
        functools.partial(terms_kernel, rows, len(sides), tile),
        in_specs=[pl.BlockSpec(memory_space=pltpu.VMEM)] * len(operands),
        out_specs=pl.BlockSpec(memory_space=pltpu.VMEM),
        out_shape=jax.ShapeDtypeStruct((count, width), jnp.float32),
        scratch_shapes=[pltpu.VMEM((2, count, tokens), jnp.bfloat16)] * len(sides),
        compiler_params=pltpu.CompilerParams(vmem_limit_bytes=32 * 2**20),
        cost_estimate=pl.CostEstimate(
            flops=4 * len(sides) * count * tokens * width,
            bytes_accessed=8 * tokens * width,
            transcendentals=0,
        ),
        name="terms",
    )(*operands)


def step_kernel(g_ref, *refs):
    state_refs, out_refs, (made, grad_ref, out_sems) = refs[:3], refs[3:6], refs[6:]
    rows, width = grad_ref.shape[0] // PROJ, grad_ref.shape[1]

    def part(k):
        return slice(None), slice(k * width, (k + 1) * width)

    def leaving(n, k):
        return pltpu.make_async_copy(made.at[n, k], out_refs[n].at[part(k)], out_sems.at[n, k])

    shape = (PROJ * rows, g_ref.shape[0])
    m = lax.broadcasted_iota(jnp.int32, shape, 0)
    j = lax.broadcasted_iota(jnp.int32, shape, 1)
    coarse = g_ref[...].astype(jnp.bfloat16)
    fine = (g_ref[...] - coarse.astype(jnp.float32)).astype(jnp.bfloat16)
    for at in range(2):
        wanted = j == 2 * PROJ * (m & 15) + PROJ * at + (m >> 4)
        pick = jnp.where(wanted, 1.0, 0.0).astype(jnp.bfloat16)
        total = jnp.dot(pick, coarse, preferred_element_type=jnp.float32)
        total += jnp.dot(pick, fine, preferred_element_type=jnp.float32)
        grad_ref[:, at * width // 2 : (at + 1) * width // 2] = total
    for k in range(PROJ):
        gradient = grad_ref[k * rows : (k + 1) * rows]
        stepped, new_moment, new_second = adam_update(
            gradient, *(ref[part(k)] for ref in state_refs)
        )
        made[1, k] = new_moment
        leaving(1, k).start()
        made[2, k] = new_second
        leaving(2, k).start()
        scale = jnp.sqrt(jnp.sum(stepped * stepped, axis=1, keepdims=True) + 1e-06)
        made[0, k] = stepped * (1.0 / scale)
        leaving(0, k).start()
    for k in range(PROJ):
        for n in range(3):
            leaving(n, k).wait()


def step(g, master, moment, second):
    rows, width = master.shape
    width //= PROJ
    anywhere = pl.BlockSpec(memory_space=pl.ANY)
    return pl.pallas_call(
        step_kernel,
        in_specs=[pl.BlockSpec(memory_space=pltpu.VMEM)] * 4,
        out_specs=[anywhere] * 3,
        out_shape=[jax.ShapeDtypeStruct(master.shape, jnp.float32)] * 3,
        scratch_shapes=[
            pltpu.VMEM((3, PROJ, rows, width), jnp.float32),
            pltpu.VMEM((PROJ * rows, width), jnp.float32),
            pltpu.SemaphoreType.DMA((3, PROJ)),
        ],
        compiler_params=pltpu.CompilerParams(vmem_limit_bytes=28 * 2**20),
        cost_estimate=pl.CostEstimate(
            flops=20 * 64 * width, bytes_accessed=24 * rows * width * PROJ, transcendentals=0
        ),
        name="step",
    )(g, master, moment, second)


def lay_kernel(place_ref, own_ref, other_ref, out_ref, held_ref, sems):
    slots, tile = sems.shape[0], held_ref.shape[3]
    mine, half = own_ref.shape[1] // 2, own_ref.shape[2]
    parts = own_ref.shape[0] * mine
    m = lax.broadcasted_iota(jnp.int32, (parts, parts), 0)
    n = lax.broadcasted_iota(jnp.int32, (parts, parts), 1)
    ahead = ((m >> 4) - place_ref[1]) & 3
    wanted = n == (m & 15) * 16 + ahead * 4 + (m >> 6)
    pick = jnp.where(wanted, 1.0 / UNIT_SCALE, 0.0).astype(jnp.bfloat16)

    def leaving(j, k):
        at = slice(k * 2 * half + j * tile, k * 2 * half + (j + 1) * tile)
        return pltpu.make_async_copy(
            held_ref.at[j % slots, k], out_ref.at[:, at], sems.at[j % slots, k]
        )

    steps = 2 * half // tile
    for j in range(steps):
        if j >= slots:
            for k in range(PROJ):
                leaving(j - slots, k).wait()
        side, at = divmod(j * tile, half)
        for ref, core in ((own_ref, place_ref[0]), (other_ref, 1 - place_ref[0])):
            values = ref[:, side * mine : (side + 1) * mine, at : at + tile].reshape(parts, tile)
            rows = jnp.dot(pick, values, preferred_element_type=jnp.float32).astype(out_ref.dtype)
            for k in range(PROJ):
                for zl in range(NZL):
                    to = pl.ds(pl.multiple_of(32 * zl + 16 * core, 16), 16)
                    start = 64 * k + 16 * zl
                    held_ref[j % slots, k, to] = rows[start : start + 16]
        for k in range(PROJ):
            leaving(j, k).start()
    for j in range(max(steps - slots, 0), steps):
        for k in range(PROJ):
            leaving(j, k).wait()


def lay(place, own, other, rows, tile=768, slots=4):
    width = 2 * own.shape[2]
    return pl.pallas_call(
        lay_kernel,
        in_specs=[pl.BlockSpec(memory_space=pltpu.SMEM)]
        + [pl.BlockSpec(memory_space=pltpu.VMEM)] * 2,
        out_specs=pl.BlockSpec(memory_space=pl.ANY),
        out_shape=jax.ShapeDtypeStruct((rows, PROJ * width), jnp.bfloat16),
        scratch_shapes=[
            pltpu.VMEM((slots, PROJ, rows, tile), jnp.bfloat16),
            pltpu.SemaphoreType.DMA((slots, PROJ)),
        ],
        compiler_params=pltpu.CompilerParams(vmem_limit_bytes=28 * 2**20),
        cost_estimate=pl.CostEstimate(
            flops=2 * 256 * own.size, bytes_accessed=4 * own.size, transcendentals=0
        ),
        name="lay",
    )(place, own, other)


def shards(x_in, attn_out, grads_out, master, moment, second):
    width = x_in.shape[1]
    swap = [(0, 1), (1, 0)]
    core = lax.axis_index("c")
    place = jnp.stack([lax.axis_index(name) for name in ("c", "zl", "x", "y")]).astype(jnp.int32)
    half = width // 2

    def ahead(a, by):
        ring = NZH * NZL
        return lax.ppermute(a, ("zh", "zl"), [(z, (z + by) % ring) for z in range(ring)])

    def opposite(a):
        ring = NZH * NZL
        pairs = [
            (z * NC + c, (z + (2 if c == 0 else ring - 2)) % ring * NC + c)
            for z in range(ring)
            for c in range(NC)
        ]
        return lax.ppermute(a, ("zh", "zl", "c"), pairs)

    def onward(a, by, turned):
        pairs = []
        for n in range(PLANE * NC):
            y, x, core = n // (NX * NC), n // NC % NX, n % NC
            to_y, to_x = ((y + by) % NY, x) if core != turned else (y, (x + by) % NX)
            pairs.append((n, (to_y * NX + to_x) * NC + core))
        return lax.ppermute(a, ("y", "x", "c"), pairs)

    def shared(kept, rows, turned):
        blocks = rows.astype(jnp.float16).reshape(3, -1, half)
        came = [onward(blocks[n - 1], n, turned).astype(jnp.float32) for n in (1, 3, 2)]
        return kept + came[0] + came[1] + came[2]

    def columns(a, which):
        return lax.dynamic_slice_in_dim(a, which * half, half, axis=1)

    with jax.named_scope("pair"):
        left, left_send = lefts(place, grads_out)
        left_other = lax.ppermute(left_send, "c", swap)
        x_other = lax.ppermute(columns(x_in, 1 - core), "c", swap)
        a_other = lax.ppermute(columns(attn_out, 1 - core), "c", swap)
        own = (left, columns(x_in, core), columns(attn_out, core))
        other = (left_other, x_other, a_other)
        block = grads_out.shape[1] // 4
        going, staying = slice(block, 4 * block), slice(0, block)
        sent = terms(going, other, base=terms(going, own))
    with jax.named_scope("plane_sum"):
        part = shared(terms(staying, own, other) * SEND_SCALE, sent * SEND_SCALE, 0)
        part = part * 0.25
        part = shared(part[: block // 4], part[block // 4 :], 1)
    with jax.named_scope("depth_sum"):
        part = (part * (4.0 / SEND_SCALE)).reshape(NZL, NC * PROJ, half)
        part = part[0] + ahead(part[1], 1) + ahead(part[3], 7) + opposite(part[2])
        part = part + lax.ppermute(part, "zh", swap)
        came = lax.ppermute(part, "c", swap)
        gradient = jnp.where(
            core == 0,
            jnp.concatenate([part[:PROJ], came[:PROJ]], axis=1),
            jnp.concatenate([came[PROJ:], part[PROJ:]], axis=1),
        )
    with jax.named_scope("own_row"):
        row = lax.axis_index("y") * NX + lax.axis_index("x")

        def piece(a):
            return lax.dynamic_slice(a, (row, 0), (1, PROJ * width)).reshape(PROJ, width)

        stepped, _, _ = adam_update(gradient, piece(master), piece(moment), piece(second))
        scale = jnp.sqrt(jnp.sum(stepped * stepped, axis=1, keepdims=True) + 1e-06)
        unit = (stepped / scale).astype(jnp.bfloat16)
        unit, small = (
            jnp.concatenate([a[:, :half], a[:, half:]], axis=0) for a in (unit, gradient)
        )
    with jax.named_scope("depth_gather"):
        units = [unit, ahead(unit, 7), opposite(unit), ahead(unit, 1)]
    with jax.named_scope("plane_gather"):
        order = np.arange(2 * NZL * PROJ).reshape(NZL, 2, PROJ).swapaxes(0, 1).reshape(-1)
        turn = jnp.asarray(np.eye(2 * NZL * PROJ)[order] * UNIT_SCALE, jnp.bfloat16)
        units = jnp.dot(turn, jnp.concatenate(units, axis=0), preferred_element_type=jnp.float32)
        payload = jnp.concatenate([units, small], axis=0).astype(jnp.float16)
        came = lax.all_gather(payload, ("y", "x"), axis=0, tiled=True)
        came = came.reshape(PLANE, 2 * (NZL + 1) * PROJ, half)
        grads = came[:, 2 * NZL * PROJ :].astype(jnp.float32).reshape(2 * PLANE * PROJ, half)
        own = came[:, : 2 * NZL * PROJ].astype(jnp.bfloat16)
    other = lax.ppermute(own, "c", swap)
    new_master, new_moment, new_second = step(grads, master, moment, second)
    gathered = lay(place, own, other, NZL * NC * master.shape[0])
    return (new_master, new_moment, new_second, gathered)


def solution(mesh):
    fine = Mesh(mesh.devices.reshape(NY, NX, NZH, NZL, NC), REP + SHARD)
    tokens = P(REP + SHARD, None)
    rows = P(SHARD, None)
    return jax.shard_map(
        shards,
        mesh=fine,
        in_specs=(tokens, tokens, tokens, rows, rows, rows),
        out_specs=(rows, rows, rows, P()),
        check_vma=False,
    )
```

```python
import functools

import jax
import jax.numpy as jnp
import numpy as np
from jax import lax
from jax.experimental import pallas as pl
from jax.experimental.pallas import tpu as pltpu
from jax.sharding import Mesh
from jax.sharding import PartitionSpec as P

beta_one = 0.9
beta_two = 0.95
learn_rate = 0.002
bias_one = 1.0 - 0.9**10
bias_two = 1.0 - 0.95**10

REP = ("y", "x", "zh")
SHARD = ("zl", "c")
NY, NX, NZH, NZL, NC = 4, 4, 2, 4, 2
PLANE = NY * NX
PROJ = 4
SEND_SCALE = 128.0
UNIT_SCALE = 32768.0


def adam_update(gradient, master, moment, second):
    new_moment = beta_one * moment + (1.0 - beta_one) * gradient
    new_second = beta_two * second + (1.0 - beta_two) * gradient * gradient
    stepped = master - (learn_rate / bias_one) * new_moment / (
        jnp.sqrt(new_second * (1.0 / bias_two)) + 1e-08
    )
    return (stepped, new_moment, new_second)


def lefts_kernel(place_ref, g_ref, own_ref, send_ref):
    shape = (own_ref.shape[0], g_ref.shape[1])
    m = lax.broadcasted_iota(jnp.int32, shape, 0)
    j = lax.broadcasted_iota(jnp.int32, shape, 1)
    core, depth, x, y = (place_ref[n] for n in range(4))
    first, second = m >> 7, (m >> 5) & 3
    start = 128 * ((depth + (m >> 3)) & 3) + 64 * ((m >> 2) & 1) + (m & 3)
    for out_ref, order in ((own_ref, core), (send_ref, 1 - core)):
        turn = order * (second - first)
        i = 4 * ((y + second - turn) & 3) + ((x + first + turn) & 3)
        chosen = jnp.where(j == start + 4 * i, 1.0, 0.0).astype(jnp.bfloat16)
        out_ref[...] = lax.dot_general(
            chosen, g_ref[...], (((1,), (1,)), ((), ())), preferred_element_type=jnp.float32
        ).astype(jnp.bfloat16)


def lefts(place, g):
    shape = jax.ShapeDtypeStruct((g.shape[1], g.shape[0]), g.dtype)
    return pl.pallas_call(
        lefts_kernel,
        in_specs=[pl.BlockSpec(memory_space=pltpu.SMEM), pl.BlockSpec(memory_space=pltpu.VMEM)],
        out_specs=[pl.BlockSpec(memory_space=pltpu.VMEM)] * 2,
        out_shape=[shape] * 2,
        compiler_params=pltpu.CompilerParams(vmem_limit_bytes=16 * 2**20),
        cost_estimate=pl.CostEstimate(flops=4 * g.size * g.shape[1], bytes_accessed=6 * g.size, transcendentals=0),
        name="lefts",
    )(place, g)


def mask_rows(left_ref, rows, masked_ref):
    left = left_ref[rows]
    k = lax.broadcasted_iota(jnp.int32, left.shape, 0) & 3
    masked_ref[0] = jnp.where(k < 3, left.astype(jnp.float32), 0.0).astype(left.dtype)
    masked_ref[1] = jnp.where(k == 3, left.astype(jnp.float32), 0.0).astype(left.dtype)


def terms_kernel(rows, sides, tile, *refs):
    inputs, rest = refs[: 3 * sides], refs[3 * sides :]
    bases, out_ref, masked = rest[: -1 - sides], rest[-1 - sides], rest[-sides:]
    groups = [inputs[3 * n : 3 * n + 3] for n in range(sides)]
    for (left_ref, _, _), masked_ref in zip(groups, masked):
        mask_rows(left_ref, rows, masked_ref)

    @pl.loop(0, out_ref.shape[1] // tile)
    def _(j):
        at = pl.ds(pl.multiple_of(j * tile, tile), tile)
        total = bases[0][:, at] if bases else 0.0
        for (_, x_ref, a_ref), masked_ref in zip(groups, masked):
            total += jnp.dot(masked_ref[0], x_ref[:, at], preferred_element_type=jnp.float32)
            total += jnp.dot(masked_ref[1], a_ref[:, at], preferred_element_type=jnp.float32)
        out_ref[:, at] = total


def terms(rows, *sides, base=None, tile=512):
    tokens, width = sides[0][1].shape
    count = rows.stop - rows.start
    operands = [a for side in sides for a in side] + ([] if base is None else [base])
    return pl.pallas_call(
        functools.partial(terms_kernel, rows, len(sides), tile),
        in_specs=[pl.BlockSpec(memory_space=pltpu.VMEM)] * len(operands),
        out_specs=pl.BlockSpec(memory_space=pltpu.VMEM),
        out_shape=jax.ShapeDtypeStruct((count, width), jnp.float32),
        scratch_shapes=[pltpu.VMEM((2, count, tokens), jnp.bfloat16)] * len(sides),
        compiler_params=pltpu.CompilerParams(vmem_limit_bytes=32 * 2**20),
        cost_estimate=pl.CostEstimate(
            flops=4 * len(sides) * count * tokens * width,
            bytes_accessed=8 * tokens * width,
            transcendentals=0,
        ),
        name="terms",
    )(*operands)


def step_kernel(g_ref, *refs):
    state_refs, out_refs, (made, grad_ref, out_sems) = refs[:3], refs[3:6], refs[6:]
    rows, width = grad_ref.shape[0] // PROJ, grad_ref.shape[1]

    def part(k):
        return slice(None), slice(k * width, (k + 1) * width)

    def leaving(n, k):
        return pltpu.make_async_copy(made.at[n, k], out_refs[n].at[part(k)], out_sems.at[n, k])

    shape = (PROJ * rows, g_ref.shape[0])
    m = lax.broadcasted_iota(jnp.int32, shape, 0)
    j = lax.broadcasted_iota(jnp.int32, shape, 1)
    coarse = g_ref[...].astype(jnp.bfloat16)
    fine = (g_ref[...] - coarse.astype(jnp.float32)).astype(jnp.bfloat16)
    for at in range(2):
        wanted = j == 2 * PROJ * (m & 15) + PROJ * at + (m >> 4)
        pick = jnp.where(wanted, 1.0, 0.0).astype(jnp.bfloat16)
        total = jnp.dot(pick, coarse, preferred_element_type=jnp.float32)
        total += jnp.dot(pick, fine, preferred_element_type=jnp.float32)
        grad_ref[:, at * width // 2 : (at + 1) * width // 2] = total
    for k in range(PROJ):
        gradient = grad_ref[k * rows : (k + 1) * rows]
        stepped, new_moment, new_second = adam_update(
            gradient, *(ref[part(k)] for ref in state_refs)
        )
        made[1, k] = new_moment
        leaving(1, k).start()
        made[2, k] = new_second
        leaving(2, k).start()
        scale = jnp.sqrt(jnp.sum(stepped * stepped, axis=1, keepdims=True) + 1e-06)
        made[0, k] = stepped * (1.0 / scale)
        leaving(0, k).start()
    for k in range(PROJ):
        for n in range(3):
            leaving(n, k).wait()


def step(g, master, moment, second):
    rows, width = master.shape
    width //= PROJ
    anywhere = pl.BlockSpec(memory_space=pl.ANY)
    return pl.pallas_call(
        step_kernel,
        in_specs=[pl.BlockSpec(memory_space=pltpu.VMEM)] * 4,
        out_specs=[anywhere] * 3,
        out_shape=[jax.ShapeDtypeStruct(master.shape, jnp.float32)] * 3,
        scratch_shapes=[
            pltpu.VMEM((3, PROJ, rows, width), jnp.float32),
            pltpu.VMEM((PROJ * rows, width), jnp.float32),
            pltpu.SemaphoreType.DMA((3, PROJ)),
        ],
        compiler_params=pltpu.CompilerParams(vmem_limit_bytes=28 * 2**20),
        cost_estimate=pl.CostEstimate(
            flops=20 * 64 * width, bytes_accessed=24 * rows * width * PROJ, transcendentals=0
        ),
        name="step",
    )(g, master, moment, second)


def lay_kernel(place_ref, own_ref, other_ref, out_ref, held_ref, sems):
    slots, tile = sems.shape[0], held_ref.shape[3]
    mine, half = own_ref.shape[1] // 2, own_ref.shape[2]
    parts = own_ref.shape[0] * mine
    m = lax.broadcasted_iota(jnp.int32, (parts, parts), 0)
    n = lax.broadcasted_iota(jnp.int32, (parts, parts), 1)
    ahead = ((m >> 4) - place_ref[1]) & 3
    wanted = n == (m & 15) * 16 + ahead * 4 + (m >> 6)
    pick = jnp.where(wanted, 1.0 / UNIT_SCALE, 0.0).astype(jnp.bfloat16)

    def leaving(j, k):
        at = slice(k * 2 * half + j * tile, k * 2 * half + (j + 1) * tile)
        return pltpu.make_async_copy(
            held_ref.at[j % slots, k], out_ref.at[:, at], sems.at[j % slots, k]
        )

    steps = 2 * half // tile
    for j in range(steps):
        if j >= slots:
            for k in range(PROJ):
                leaving(j - slots, k).wait()
        side, at = divmod(j * tile, half)
        for ref, core in ((own_ref, place_ref[0]), (other_ref, 1 - place_ref[0])):
            values = ref[:, side * mine : (side + 1) * mine, at : at + tile].reshape(parts, tile)
            rows = jnp.dot(pick, values, preferred_element_type=jnp.float32).astype(out_ref.dtype)
            for k in range(PROJ):
                for zl in range(NZL):
                    to = pl.ds(pl.multiple_of(32 * zl + 16 * core, 16), 16)
                    start = 64 * k + 16 * zl
                    held_ref[j % slots, k, to] = rows[start : start + 16]
        for k in range(PROJ):
            leaving(j, k).start()
    for j in range(max(steps - slots, 0), steps):
        for k in range(PROJ):
            leaving(j, k).wait()


def lay(place, own, other, rows, tile=1536, slots=4):
    width = 2 * own.shape[2]
    return pl.pallas_call(
        lay_kernel,
        in_specs=[pl.BlockSpec(memory_space=pltpu.SMEM)]
        + [pl.BlockSpec(memory_space=pltpu.VMEM)] * 2,
        out_specs=pl.BlockSpec(memory_space=pl.ANY),
        out_shape=jax.ShapeDtypeStruct((rows, PROJ * width), jnp.bfloat16),
        scratch_shapes=[
            pltpu.VMEM((slots, PROJ, rows, tile), jnp.bfloat16),
            pltpu.SemaphoreType.DMA((slots, PROJ)),
        ],
        compiler_params=pltpu.CompilerParams(vmem_limit_bytes=28 * 2**20),
        cost_estimate=pl.CostEstimate(
            flops=2 * 256 * own.size, bytes_accessed=4 * own.size, transcendentals=0
        ),
        name="lay",
    )(place, own, other)


def shards(x_in, attn_out, grads_out, master, moment, second):
    width = x_in.shape[1]
    swap = [(0, 1), (1, 0)]
    core = lax.axis_index("c")
    place = jnp.stack([lax.axis_index(name) for name in ("c", "zl", "x", "y")]).astype(jnp.int32)
    half = width // 2

    def ahead(a, by):
        ring = NZH * NZL
        return lax.ppermute(a, ("zh", "zl"), [(z, (z + by) % ring) for z in range(ring)])

    def opposite(a):
        ring = NZH * NZL
        pairs = [
            (z * NC + c, (z + (2 if c == 0 else ring - 2)) % ring * NC + c)
            for z in range(ring)
            for c in range(NC)
        ]
        return lax.ppermute(a, ("zh", "zl", "c"), pairs)

    def onward(a, by, turned):
        pairs = []
        for n in range(PLANE * NC):
            y, x, core = n // (NX * NC), n // NC % NX, n % NC
            to_y, to_x = ((y + by) % NY, x) if core != turned else (y, (x + by) % NX)
            pairs.append((n, (to_y * NX + to_x) * NC + core))
        return lax.ppermute(a, ("y", "x", "c"), pairs)

    def shared(kept, rows, turned):
        blocks = rows.astype(jnp.float16).reshape(3, -1, half)
        came = [onward(blocks[n - 1], n, turned).astype(jnp.float32) for n in (1, 3, 2)]
        return kept + came[0] + came[1] + came[2]

    def columns(a, which):
        return lax.dynamic_slice_in_dim(a, which * half, half, axis=1)

    with jax.named_scope("pair"):
        left, left_send = lefts(place, grads_out)
        left_other = lax.ppermute(left_send, "c", swap)
        x_other = lax.ppermute(columns(x_in, 1 - core), "c", swap)
        a_other = lax.ppermute(columns(attn_out, 1 - core), "c", swap)
        own = (left, columns(x_in, core), columns(attn_out, core))
        other = (left_other, x_other, a_other)
        block = grads_out.shape[1] // 4
        going, staying = slice(block, 4 * block), slice(0, block)
        sent = terms(going, other, base=terms(going, own))
    with jax.named_scope("plane_sum"):
        part = shared(terms(staying, own, other) * SEND_SCALE, sent * SEND_SCALE, 0)
        part = part * 0.25
        part = shared(part[: block // 4], part[block // 4 :], 1)
    with jax.named_scope("depth_sum"):
        part = (part * (4.0 / SEND_SCALE)).reshape(NZL, NC * PROJ, half)
        part = part[0] + ahead(part[1], 1) + ahead(part[3], 7) + opposite(part[2])
        part = part + lax.ppermute(part, "zh", swap)
        came = lax.ppermute(part, "c", swap)
        gradient = jnp.where(
            core == 0,
            jnp.concatenate([part[:PROJ], came[:PROJ]], axis=1),
            jnp.concatenate([came[PROJ:], part[PROJ:]], axis=1),
        )
    with jax.named_scope("own_row"):
        row = lax.axis_index("y") * NX + lax.axis_index("x")

        def piece(a):
            return lax.dynamic_slice(a, (row, 0), (1, PROJ * width)).reshape(PROJ, width)

        stepped, _, _ = adam_update(gradient, piece(master), piece(moment), piece(second))
        scale = jnp.sqrt(jnp.sum(stepped * stepped, axis=1, keepdims=True) + 1e-06)
        unit = (stepped / scale).astype(jnp.bfloat16)
        unit, small = (
            jnp.concatenate([a[:, :half], a[:, half:]], axis=0) for a in (unit, gradient)
        )
    with jax.named_scope("depth_gather"):
        units = [unit, ahead(unit, 7), opposite(unit), ahead(unit, 1)]
    with jax.named_scope("plane_gather"):
        order = np.arange(2 * NZL * PROJ).reshape(NZL, 2, PROJ).swapaxes(0, 1).reshape(-1)
        turn = jnp.asarray(np.eye(2 * NZL * PROJ)[order] * UNIT_SCALE, jnp.bfloat16)
        units = jnp.dot(turn, jnp.concatenate(units, axis=0), preferred_element_type=jnp.float32)
        payload = jnp.concatenate([units, small], axis=0).astype(jnp.float16)
        came = lax.all_gather(payload, ("y", "x"), axis=0, tiled=True)
        came = came.reshape(PLANE, 2 * (NZL + 1) * PROJ, half)
        grads = came[:, 2 * NZL * PROJ :].astype(jnp.float32).reshape(2 * PLANE * PROJ, half)
        own = came[:, : 2 * NZL * PROJ].astype(jnp.bfloat16)
    other = lax.ppermute(own, "c", swap)
    new_master, new_moment, new_second = step(grads, master, moment, second)
    gathered = lay(place, own, other, NZL * NC * master.shape[0])
    return (new_master, new_moment, new_second, gathered)


def solution(mesh):
    fine = Mesh(mesh.devices.reshape(NY, NX, NZH, NZL, NC), REP + SHARD)
    tokens = P(REP + SHARD, None)
    rows = P(SHARD, None)
    return jax.shard_map(
        shards,
        mesh=fine,
        in_specs=(tokens, tokens, tokens, rows, rows, rows),
        out_specs=(rows, rows, rows, P()),
        check_vma=False,
    )
```
